32 devices in a mesh: circ: 4 (over z), rad: 4 (over y, x), ax: 2 (over core).
Axes of the slice: x: 2, y: 2, z: 4, core: 2. Of those that a mesh axis runs over, the one named last changes fastest.
Arguments:
- state: float32 [5, 16, 32, 512], P(None, 'ax', 'rad', 'circ'), may hold values from -6 to 6
- eddy: float32 [16, 32, 512], P('ax', 'rad', 'circ'), may hold values from 0.02 to 0.2
- offsets: int32 [4], replicated, may hold values from 0 to 3, as said below
- stencil_index: int32 [2, 4, 128, 4], replicated, may hold values from 0 to 127
- stencil_weight: float32 [2, 4, 128, 4], replicated, may hold values from 0.1 to 1
Outputs:
- advanced: float32 [5, 16, 32, 512], P(None, 'ax', 'rad', 'circ')
The draws below stay inside these ranges and needn't reach their ends.
Inputs may be any that keep to these rules, and one draw needn't show every extreme that they name: Among the sections' offsets are 2, 3 and 0.
All inputs are finite; a program needn't handle non-finite values.
Results may differ from the reference program's by a relative error of at most 0.00005.
Values sent between devices are 32-bit elements; how exact they have to be, the bound alone decides.
A program may use at most 64 MiB of HBM per device.

```python
import math
import jax
import jax.numpy as jnp
from jax import lax

NV = 5
SECTIONS = 4
TAPS = 4
CC = 128
CA = 8
NC = 512
NR = 32
NA = 16
N_CIRC = 4


def draw_offsets(key, part):
    values = jax.random.randint(jax.random.fold_in(key, 11), (SECTIONS,), 0, N_CIRC, dtype=jnp.int32)
    chosen = jax.random.randint(jax.random.fold_in(key, 12), (), 0, SECTIONS, dtype=jnp.int32)
    section_ids = jnp.arange(SECTIONS, dtype=jnp.int32)
    after_one = (chosen + 1) % SECTIONS
    after_two = (chosen + 2) % SECTIONS
    values = jnp.where(section_ids == after_two, jnp.int32(0), values)
    values = jnp.where(section_ids == after_one, jnp.int32(N_CIRC - 1), values)
    values = jnp.where(section_ids == chosen, jnp.int32(N_CIRC // 2), values)
    return values.astype(jnp.int32)


def set_ends(values, key, least, largest):
    place = [jax.random.randint(jax.random.fold_in(key, axis), (), 0, length) for axis, length in enumerate(values.shape)]
    widest = values.shape.index(max(values.shape))
    neighbour = place[:widest] + [(place[widest] + 1) % values.shape[widest]] + place[widest + 1:]
    return values.at[tuple(place)].set(least).at[tuple(neighbour)].set(largest)


def shard_levels(key, shape, shards, least, top_value):
    gain, own = 1.0, jax.random.fold_in(key, 6)
    for axis_at, parts in shards:
        steps = jnp.exp(jax.random.uniform(jax.random.fold_in(own, axis_at), (parts,), jnp.float32, least / len(shards), top_value / len(shards)))
        gain = gain * jnp.repeat(steps, shape[axis_at] // parts).reshape([-1 if axis == axis_at else 1 for axis in range(len(shape))])
    return gain


def bell_draw(rng, extent, scale, most, pieces=(), kind=jnp.bfloat16):
    gain = shard_levels(rng, extent, pieces, -0.22, 0.18) if pieces else 1.0
    drawn = jax.random.normal(rng, extent, jnp.float32) * scale * gain
    return jnp.minimum(jnp.maximum(drawn, -most), most).astype(kind)


def setup_inputs(seed: int = 0) -> dict:
    splits = jax.random.split(jax.random.key(seed), 6)
    state = bell_draw(splits[0], (NV, NA, NR, NC), 1.0, 6.0, ((1, 2), (2, 4), (3, 4)), jnp.float32)
    eddy = jnp.clip(jnp.exp(math.log(0.2) - 2.3025851 * jax.random.uniform(splits[1], (NA, NR, NC), jnp.float32) ** shard_levels(splits[1], (NA, NR, NC), ((0, 2), (1, 4), (2, 4)), -0.2, 0.2)), 0.02, 0.2)
    offsets = draw_offsets(jax.random.fold_in(splits[5], 71), 0)
    stencil_index = set_ends(jax.random.randint(splits[3], (2, SECTIONS, CC, TAPS), 0, CC), jax.random.fold_in(splits[3], 1), 0, CC - 1).astype(jnp.int32)
    stencil_weight = jnp.clip(jax.random.uniform(splits[4], (2, SECTIONS, CC, TAPS), jnp.float32, 0.1, 1.0), 0.1, 1.0)
    return dict(state=state, eddy=eddy, offsets=offsets, stencil_index=stencil_index, stencil_weight=stencil_weight)


AXIAL_MACH = 0.4
STEP_SIZE = 0.3


def interp_matrix(index_rows, weight_rows):
    width = index_rows.shape[0]
    onehot = (index_rows[:, :, None] == jnp.arange(width, dtype=jnp.int32)[None, None, :]).astype(jnp.float32)
    normed = weight_rows / jnp.sum(weight_rows, axis=1, keepdims=True)
    return jnp.sum(normed[:, :, None] * onehot, axis=1)


def tendency(center, circ_low, circ_high, radial_low, radial_high, axial_low, axial_high, swirl, eddy):
    diff_circ = 0.5 * (circ_high - circ_low)
    diff_radial = 0.5 * (radial_high - radial_low)
    diff_axial = 0.5 * (axial_high - axial_low)
    laplace = (circ_high + circ_low) + (radial_high + radial_low) + (axial_high + axial_low) - 6.0 * center
    advect = swirl * diff_circ + AXIAL_MACH * diff_axial
    diverge = diff_circ[1] + diff_radial[2] + diff_axial[3]
    flux = jnp.stack([diverge, diff_circ[4], diff_radial[4], diff_axial[4], diverge])
    return -advect - flux + eddy[None] * laplace


def interpolate(plane, matrix):
    width = matrix.shape[0]
    flat_rows = plane.reshape(-1, width)
    out = jnp.dot(flat_rows, matrix.T, precision=lax.Precision.HIGHEST, preferred_element_type=jnp.float32)
    return out.reshape(plane.shape)


def section_tendency(field, eddy, offset_now, index_section, weight_section):
    sectors = N_CIRC
    nvar, naxial, nradial, ncirc = field.shape
    stator_plane = field[:, CA - 1].reshape(nvar, nradial, sectors, CC)
    rotor_plane = field[:, CA].reshape(nvar, nradial, sectors, CC)
    cycle = jnp.arange(sectors, dtype=jnp.int32)
    facing_rotor = stator_plane[:, :, (cycle + offset_now) % sectors]
    facing_stator = rotor_plane[:, :, (cycle + sectors - offset_now) % sectors]
    rotor_ghost = interpolate(facing_rotor, interp_matrix(index_section[1], weight_section[1])).reshape(nvar, nradial, ncirc)
    stator_ghost = interpolate(facing_stator, interp_matrix(index_section[0], weight_section[0])).reshape(nvar, nradial, ncirc)
    circ_low = jnp.roll(field, 1, axis=3)
    circ_high = jnp.roll(field, -1, axis=3)
    zero_row = jnp.zeros((nvar, naxial, 1, ncirc), jnp.float32)
    radial_low = jnp.concatenate([zero_row, field[:, :, :-1]], axis=2)
    radial_high = jnp.concatenate([field[:, :, 1:], zero_row], axis=2)
    zero_plane = jnp.zeros((nvar, 1, nradial, ncirc), jnp.float32)
    results = []
    for half in range(2):
        lower = half * CA
        block = field[:, lower:lower + CA]
        if half == 0:
            below, above, swirl = zero_plane, stator_ghost[:, None], 0.2
        else:
            below, above, swirl = rotor_ghost[:, None], zero_plane, -0.3
        axial_low = jnp.concatenate([below, block[:, :-1]], axis=1)
        axial_high = jnp.concatenate([block[:, 1:], above], axis=1)
        results.append(tendency(block, circ_low[:, lower:lower + CA], circ_high[:, lower:lower + CA],
                                radial_low[:, lower:lower + CA], radial_high[:, lower:lower + CA],
                                axial_low, axial_high, swirl, eddy[lower:lower + CA]))
    return jnp.concatenate(results, axis=1)


def reference(state, eddy, offsets, stencil_index, stencil_weight):
    def slope(field, section):
        return section_tendency(field, eddy, offsets[section], stencil_index[:, section], stencil_weight[:, section])

    slope_one = slope(state, 0)
    slope_two = slope(state + (0.5 * STEP_SIZE) * slope_one, 1)
    slope_three = slope(state + (0.5 * STEP_SIZE) * slope_two, 2)
    slope_four = slope(state + STEP_SIZE * slope_three, 3)
    return state + (STEP_SIZE / 6.0) * (slope_one + 2.0 * slope_two + 2.0 * slope_three + slope_four)
```

```python
import functools

import jax
import jax.numpy as jnp
from jax import lax
from jax.experimental import pallas as pl
from jax.experimental.pallas import tpu as pltpu
from jax.sharding import PartitionSpec as P

AXIAL_MACH = 0.4
STEP_SIZE = 0.3
MESH = pl.DeviceIdType.MESH
STAGE = (0.5 * STEP_SIZE, 0.5 * STEP_SIZE, STEP_SIZE)
BLEND = (1.0, 2.0, 2.0, 1.0)


def build_table(index, weight):
    taps, width = index.shape
    normed = weight / jnp.sum(weight, axis=0, keepdims=True)
    source = lax.broadcasted_iota(jnp.int32, (width, width), 0)
    matrix = jnp.zeros((width, width), jnp.float32)
    for tap in range(taps):
        matrix += jnp.where(index[tap : tap + 1] == source, normed[tap : tap + 1], 0.0)
    high = matrix.astype(jnp.bfloat16)
    low = (matrix - high.astype(jnp.float32)).astype(jnp.bfloat16)
    top = jnp.concatenate([high, low], axis=1)
    bottom = jnp.concatenate([high, jnp.zeros_like(high)], axis=1)
    return jnp.concatenate([top, bottom], axis=0)


def interpolate(plane, table):
    width = plane.shape[1]
    high = plane.astype(jnp.bfloat16)
    low = (plane - high.astype(jnp.float32)).astype(jnp.bfloat16)
    both = jnp.dot(
        jnp.concatenate([high, low], axis=1), table, preferred_element_type=jnp.float32
    )
    return both[:, :width] + both[:, width:]


def kernel(
    n_circ, n_rad,
    state_ref, eddy_ref, offset_ref, index_ref, weight_ref, out_ref,
    field, total, table, plane_out, rad_out, rad_in, circ_out, circ_in,
    plane_send, plane_recv, rad_send, rad_recv, circ_send, circ_recv, *plane_in,
):
    nvar, naxial, nradial, width = state_ref.shape
    sections = offset_ref.shape[0]
    rows = nvar * nradial
    tiles = nvar * naxial
    circ, rad, ax = lax.axis_index("circ"), lax.axis_index("rad"), lax.axis_index("ax")
    far = 1 - ax
    circ_up, circ_down = lax.rem(circ + 1, n_circ), lax.rem(circ + n_circ - 1, n_circ)
    has_low, has_high = rad > 0, rad < n_rad - 1
    front = jnp.where(ax == 0, naxial - 1, 0)
    front_rows = pl.ds(pl.multiple_of(front * rows, 8), rows)

    barrier = pltpu.get_barrier_semaphore()

    def greet(device):
        pl.semaphore_signal(barrier, inc=1, device_id=device, device_id_type=MESH)

    for apart in range(n_circ):
        greet((lax.rem(circ + apart, n_circ), rad, far))
    greet((circ_up, rad, ax))
    greet((circ_down, rad, ax))

    @pl.when(has_low)
    def _():
        greet((circ, rad - 1, ax))

    @pl.when(has_high)
    def _():
        greet((circ, rad + 1, ax))

    for a in range(naxial):
        field[0, a * rows : (a + 1) * rows, :] = state_ref[:, a].reshape(rows, width)

    @pl.when(jnp.logical_not(has_low))
    def _():
        for s in range(sections):
            rad_in[s, 0] = jnp.zeros((tiles, width), jnp.float32)

    @pl.when(jnp.logical_not(has_high))
    def _():
        for s in range(sections):
            rad_in[s, 1] = jnp.zeros((tiles, width), jnp.float32)

    pl.semaphore_wait(
        barrier, n_circ + 2 + jnp.where(has_low, 1, 0) + jnp.where(has_high, 1, 0)
    )

    def plane_copy(s, apart):
        return pltpu.make_async_remote_copy(
            src_ref=plane_out.at[s], dst_ref=plane_in[s].at[circ],
            send_sem=plane_send.at[s, apart], recv_sem=plane_recv.at[s, circ],
            device_id=(lax.rem(circ + apart, n_circ), rad, far), device_id_type=MESH,
        )

    def plane_arrival(s, source):
        return pltpu.make_async_remote_copy(
            src_ref=plane_out.at[s], dst_ref=plane_in[s].at[source],
            send_sem=plane_send.at[s, 0], recv_sem=plane_recv.at[s, source],
            device_id=(source, rad, far), device_id_type=MESH,
        )

    def circ_copy(s, side):
        return pltpu.make_async_remote_copy(
            src_ref=circ_out.at[s, side], dst_ref=circ_in.at[s, side],
            send_sem=circ_send.at[s, side], recv_sem=circ_recv.at[s, side],
            device_id=(circ_up if side == 0 else circ_down, rad, ax), device_id_type=MESH,
        )

    def rad_copy(s, side):
        return pltpu.make_async_remote_copy(
            src_ref=rad_out.at[s, side], dst_ref=rad_in.at[s, side],
            send_sem=rad_send.at[s, side], recv_sem=rad_recv.at[s, side],
            device_id=(circ, rad + 1 if side == 0 else rad - 1, ax), device_id_type=MESH,
        )

    sends_rad = (has_high, has_low)
    gets_rad = (has_low, has_high)
    lane = lax.broadcasted_iota(jnp.int32, (nvar, nradial, width), 2)
    sub = lax.broadcasted_iota(jnp.int32, (nvar, nradial, width), 1)
    swirl = jnp.where(ax == 1, -0.3, 0.2).astype(jnp.float32)
    toward = jnp.where(ax == 1, -0.5, 0.5).astype(jnp.float32)
    wide = lax.broadcasted_iota(jnp.int32, (tiles, nradial, width), 2)
    tile_of = lax.broadcasted_iota(jnp.int32, (tiles, nradial, width), 0)

    for s in range(sections):
        last = s == sections - 1
        plane_out[s] = field[s, front_rows, :]
        for apart in reversed(range(n_circ)):
            plane_copy(s, apart).start()

        cells = field[s].reshape(tiles, nradial, width)
        for side, edge in ((0, width - 1), (1, 0)):
            column = jnp.broadcast_to(cells[:, :, edge : edge + 1], cells.shape)
            circ_out[s, side] = jnp.sum(jnp.where(wide == tile_of, column, 0.0), axis=0)
            circ_copy(s, side).start()
        for side, edge in ((0, nradial - 1), (1, 0)):
            rad_out[s, side] = field[s, pl.ds(edge, tiles, stride=nradial), :]

            @pl.when(sends_rad[side])
            def _():
                rad_copy(s, side).start()

        table[s] = build_table(index_ref[ax, s], weight_ref[ax, s])

        for side in range(2):
            circ_copy(s, side).wait_recv()

            @pl.when(gets_rad[side])
            def _():
                rad_copy(s, side).wait_recv()

        circ_low_edge, circ_high_edge = circ_in[s, 0], circ_in[s, 1]

        def spread(edges, a):
            picked = [
                jnp.broadcast_to(edges[:, t : t + 1], (nradial, width))
                for t in range(a * nvar, (a + 1) * nvar)
            ]
            return jnp.stack(picked)

        def spread_rows(side, a):
            picked = rad_in[s, side, a * nvar : (a + 1) * nvar, :]
            return jnp.broadcast_to(picked[:, None, :], (nvar, nradial, width))

        def plane_at(a):
            return field[s, a * rows : (a + 1) * rows, :].reshape(nvar, nradial, width)

        zero = jnp.zeros((nvar, nradial, width), jnp.float32)
        for a in range(naxial):
            q = plane_at(a)
            axial_low = plane_at(a - 1) if a > 0 else zero
            axial_high = plane_at(a + 1) if a < naxial - 1 else zero
            circ_low = jnp.where(lane == 0, spread(circ_low_edge, a), pltpu.roll(q, 1, 2))
            circ_high = jnp.where(
                lane == width - 1, spread(circ_high_edge, a), pltpu.roll(q, width - 1, 2)
            )
            rad_low = jnp.where(sub == 0, spread_rows(0, a), pltpu.roll(q, 1, 1))
            rad_high = jnp.where(
                sub == nradial - 1, spread_rows(1, a), pltpu.roll(q, nradial - 1, 1)
            )
            diff_circ = 0.5 * (circ_high - circ_low)
            diff_axial = 0.5 * (axial_high - axial_low)
            laplace = (
                (circ_high + circ_low) + (rad_high + rad_low) + (axial_high + axial_low) - 6.0 * q
            )
            slope = eddy_ref[a][None] * laplace - (swirl * diff_circ + AXIAL_MACH * diff_axial)
            diff_rad_2 = 0.5 * (rad_high[2] - rad_low[2])
            diff_rad_4 = 0.5 * (rad_high[4] - rad_low[4])
            diverge = diff_circ[1] + diff_rad_2 + diff_axial[3]
            flux = jnp.stack([diverge, diff_circ[4], diff_rad_4, diff_axial[4], diverge])
            slope = slope - flux
            base = state_ref[:, a]
            if s == 0:
                total[:, a] = slope
            else:
                total[:, a] += BLEND[s] * slope
            if not last:
                field[s + 1, a * rows : (a + 1) * rows, :] = (base + STAGE[s] * slope).reshape(
                    rows, width
                )

        for source in range(n_circ):
            plane_arrival(s, source).wait_recv()
        shift = jnp.where(ax == 1, offset_ref[s], n_circ - offset_ref[s])
        faced = plane_in[s][lax.rem(circ + shift, n_circ)]
        ghost = interpolate(faced, table[s]).reshape(nvar, nradial, width)
        slant = toward * ghost
        slope = eddy_ref[front][None] * ghost - AXIAL_MACH * slant
        none = jnp.zeros_like(slant[0])
        slope = slope - jnp.stack([slant[3], none, none, slant[4], slant[3]])
        total[:, front] += BLEND[s] * slope
        if not last:
            field[s + 1, front_rows, :] += (STAGE[s] * slope).reshape(rows, width)

    for a in range(naxial):
        out_ref[:, a] = state_ref[:, a] + (STEP_SIZE / 6.0) * total[:, a]

    for s in range(sections):
        for apart in range(n_circ):
            plane_copy(s, apart).wait_send()
        for side in range(2):
            circ_copy(s, side).wait_send()

            @pl.when(sends_rad[side])
            def _():
                rad_copy(s, side).wait_send()


def solution(mesh):
    n_circ, n_rad = mesh.shape["circ"], mesh.shape["rad"]

    def local(state, eddy, offsets, stencil_index, stencil_weight):
        nvar, naxial, nradial, width = state.shape
        sections = offsets.shape[0]
        rows, tiles = nvar * nradial, nvar * naxial
        vmem = pl.BlockSpec(memory_space=pltpu.VMEM)
        buffer = lambda *shape: pltpu.VMEM(shape, jnp.float32)
        return pl.pallas_call(
            functools.partial(kernel, n_circ, n_rad),
            out_shape=jax.ShapeDtypeStruct(state.shape, jnp.float32),
            in_specs=[vmem, vmem, pl.BlockSpec(memory_space=pltpu.SMEM), vmem, vmem],
            out_specs=vmem,
            scratch_shapes=[
                buffer(sections, rows * naxial, width),
                buffer(*state.shape),
                pltpu.VMEM((sections, 2 * width, 2 * width), jnp.bfloat16),
                buffer(sections, rows, width),
                buffer(sections, 2, tiles, width),
                buffer(sections, 2, tiles, width),
                buffer(sections, 2, nradial, width),
                buffer(sections, 2, nradial, width),
                pltpu.SemaphoreType.DMA((sections, n_circ)),
                pltpu.SemaphoreType.DMA((sections, n_circ)),
                pltpu.SemaphoreType.DMA((sections, 2)),
                pltpu.SemaphoreType.DMA((sections, 2)),
                pltpu.SemaphoreType.DMA((sections, 2)),
                pltpu.SemaphoreType.DMA((sections, 2)),
                *[buffer(n_circ, rows, width) for _ in range(sections)],
            ],
            compiler_params=pltpu.CompilerParams(
                collective_id=0, has_side_effects=True, vmem_limit_bytes=32 * 1024 * 1024
            ),
        )(state, eddy, offsets, jnp.swapaxes(stencil_index, 2, 3), jnp.swapaxes(stencil_weight, 2, 3))

    return jax.shard_map(
        local,
        mesh=mesh,
        in_specs=(P(None, "ax", "rad", "circ"), P("ax", "rad", "circ"), P(), P(), P()),
        out_specs=P(None, "ax", "rad", "circ"),
        check_vma=False,
    )
```

```python
import functools

import jax
import jax.numpy as jnp
from jax import lax
from jax.experimental import pallas as pl
from jax.experimental.pallas import tpu as pltpu
from jax.sharding import PartitionSpec as P

AXIAL_MACH = 0.4
STEP_SIZE = 0.3
MESH = pl.DeviceIdType.MESH
STAGE = (0.5 * STEP_SIZE, 0.5 * STEP_SIZE, STEP_SIZE)
BLEND = (1.0, 2.0, 2.0, 1.0)


def build_table(index, weight):
    taps, width = index.shape
    normed = weight / jnp.sum(weight, axis=0, keepdims=True)
    source = lax.broadcasted_iota(jnp.int32, (width, width), 0)
    matrix = jnp.zeros((width, width), jnp.float32)
    for tap in range(taps):
        matrix += jnp.where(index[tap : tap + 1] == source, normed[tap : tap + 1], 0.0)
    high = matrix.astype(jnp.bfloat16)
    low = (matrix - high.astype(jnp.float32)).astype(jnp.bfloat16)
    top = jnp.concatenate([high, low], axis=1)
    bottom = jnp.concatenate([high, jnp.zeros_like(high)], axis=1)
    return jnp.concatenate([top, bottom], axis=0)


def interpolate(plane, table):
    width = plane.shape[1]
    high = plane.astype(jnp.bfloat16)
    low = (plane - high.astype(jnp.float32)).astype(jnp.bfloat16)
    both = jnp.dot(
        jnp.concatenate([high, low], axis=1), table, preferred_element_type=jnp.float32
    )
    return both[:, :width] + both[:, width:]


def kernel(
    n_circ, n_rad,
    state_hbm, eddy_hbm, offset_hbm, index_hbm, weight_hbm, out_ref,
    state_ref, eddy_ref, offset_ref, index_ref, weight_ref,
    field, total, table, plane_out, rad_bulk_out, rad_bulk_in, rad_front_out, rad_front_in,
    circ_out, circ_in,
    load_sem, plane_send, plane_recv, rad_send, rad_recv, circ_send, circ_recv, *plane_in,
):
    nvar, naxial, nradial, width = state_ref.shape
    sections = offset_ref.shape[0]
    rows = nvar * nradial
    inner = naxial - 1
    circ, rad, ax = lax.axis_index("circ"), lax.axis_index("rad"), lax.axis_index("ax")
    far = 1 - ax
    circ_up, circ_down = lax.rem(circ + 1, n_circ), lax.rem(circ + n_circ - 1, n_circ)
    has_low, has_high = rad > 0, rad < n_rad - 1

    loads = [
        pltpu.make_async_copy(source, target, load_sem.at[i])
        for i, (source, target) in enumerate(
            (
                (state_hbm, state_ref),
                (eddy_hbm, eddy_ref),
                (offset_hbm, offset_ref),
                (index_hbm.at[ax], index_ref),
                (weight_hbm.at[ax], weight_ref),
            )
        )
    ]
    for load in loads:
        load.start()

    barrier = pltpu.get_barrier_semaphore()

    def greet(device):
        pl.semaphore_signal(barrier, inc=1, device_id=device, device_id_type=MESH)

    for apart in range(n_circ):
        greet((lax.rem(circ + apart, n_circ), rad, far))
    greet((circ_up, rad, ax))
    greet((circ_down, rad, ax))

    @pl.when(has_low)
    def _():
        greet((circ, rad - 1, ax))

    @pl.when(has_high)
    def _():
        greet((circ, rad + 1, ax))

    for side, missing in ((0, jnp.logical_not(has_low)), (1, jnp.logical_not(has_high))):

        @pl.when(missing)
        def _():
            for s in range(sections):
                rad_bulk_in[s, side] = jnp.zeros((inner * nvar, width), jnp.float32)
                rad_front_in[s, side] = jnp.zeros((nvar, width), jnp.float32)

    def axial(j):
        return jnp.where(ax == 0, j, naxial - 1 - j)

    def place(j):
        return pl.ds(j * rows, rows)

    def plane_at(s, j):
        return field[s, place(j), :].reshape(nvar, nradial, width)

    for load in loads:
        load.wait()
    for j in range(naxial):
        field[0, place(j), :] = state_ref[:, axial(j)].reshape(rows, width)
    plane_out[0] = field[0, place(inner), :]

    def plane_copy(s, apart):
        return pltpu.make_async_remote_copy(
            src_ref=plane_out.at[s], dst_ref=plane_in[s].at[circ],
            send_sem=plane_send.at[s, apart], recv_sem=plane_recv.at[s, circ],
            device_id=(lax.rem(circ + apart, n_circ), rad, far), device_id_type=MESH,
        )

    def plane_arrival(s, source):
        return pltpu.make_async_remote_copy(
            src_ref=plane_out.at[s], dst_ref=plane_in[s].at[source],
            send_sem=plane_send.at[s, 0], recv_sem=plane_recv.at[s, source],
            device_id=(source, rad, far), device_id_type=MESH,
        )

    def circ_copy(s, part, side):
        return pltpu.make_async_remote_copy(
            src_ref=circ_out.at[s, part, side], dst_ref=circ_in.at[s, part, side],
            send_sem=circ_send.at[s, part, side], recv_sem=circ_recv.at[s, part, side],
            device_id=(circ_up if side == 0 else circ_down, rad, ax), device_id_type=MESH,
        )

    rad_outs, rad_ins = (rad_bulk_out, rad_front_out), (rad_bulk_in, rad_front_in)

    def rad_copy(s, part, side):
        return pltpu.make_async_remote_copy(
            src_ref=rad_outs[part].at[s, side], dst_ref=rad_ins[part].at[s, side],
            send_sem=rad_send.at[s, part, side], recv_sem=rad_recv.at[s, part, side],
            device_id=(circ, rad + 1 if side == 0 else rad - 1, ax), device_id_type=MESH,
        )

    sends_rad = (has_high, has_low)
    gets_rad = (has_low, has_high)
    spans = ((0, inner), (inner, naxial))

    def send_halos(s, part):
        first, stop = spans[part]
        tiles = (stop - first) * nvar
        cells = field[s, first * rows : stop * rows, :].reshape(tiles, nradial, width)
        lane_of = lax.broadcasted_iota(jnp.int32, cells.shape, 2)
        tile_of = lax.broadcasted_iota(jnp.int32, cells.shape, 0)
        for side, edge in ((0, width - 1), (1, 0)):
            column = jnp.broadcast_to(cells[:, :, edge : edge + 1], cells.shape)
            circ_out[s, part, side] = jnp.sum(jnp.where(lane_of == tile_of, column, 0.0), axis=0)
            circ_copy(s, part, side).start()
        for side, edge in ((0, nradial - 1), (1, 0)):
            start = first * rows + edge
            rad_outs[part][s, side] = field[s, pl.ds(start, tiles, stride=nradial), :]

            @pl.when(sends_rad[side])
            def _():
                rad_copy(s, part, side).start()

    def await_halos(s, part):
        for side in range(2):
            circ_copy(s, part, side).wait_recv()

            @pl.when(gets_rad[side])
            def _():
                rad_copy(s, part, side).wait_recv()

    lane = lax.broadcasted_iota(jnp.int32, (nvar, nradial, width), 2)
    sub = lax.broadcasted_iota(jnp.int32, (nvar, nradial, width), 1)
    zero = jnp.zeros((nvar, nradial, width), jnp.float32)
    swirl = jnp.where(ax == 1, -0.3, 0.2).astype(jnp.float32)
    toward = jnp.where(ax == 1, -0.5, 0.5).astype(jnp.float32)

    def slope_at(s, j, part, edges):
        first = (j - spans[part][0]) * nvar

        def spread(side):
            return jnp.stack(
                [
                    jnp.broadcast_to(edges[side][:, t : t + 1], (nradial, width))
                    for t in range(first, first + nvar)
                ]
            )

        def spread_rows(side):
            picked = rad_ins[part][s, side, first : first + nvar, :]
            return jnp.broadcast_to(picked[:, None, :], (nvar, nradial, width))

        q = plane_at(s, j)
        before = plane_at(s, j - 1) if j > 0 else zero
        after = plane_at(s, j + 1) if j < inner else zero
        circ_low = jnp.where(lane == 0, spread(0), pltpu.roll(q, 1, 2))
        circ_high = jnp.where(lane == width - 1, spread(1), pltpu.roll(q, width - 1, 2))
        rad_low = jnp.where(sub == 0, spread_rows(0), pltpu.roll(q, 1, 1))
        rad_high = jnp.where(sub == nradial - 1, spread_rows(1), pltpu.roll(q, nradial - 1, 1))
        diff_circ = 0.5 * (circ_high - circ_low)
        diff_axial = toward * (after - before)
        laplace = (circ_high + circ_low) + (rad_high + rad_low) + (after + before) - 6.0 * q
        slope = eddy_ref[axial(j)][None] * laplace - (swirl * diff_circ + AXIAL_MACH * diff_axial)
        diverge = diff_circ[1] + 0.5 * (rad_high[2] - rad_low[2]) + diff_axial[3]
        push = 0.5 * (rad_high[4] - rad_low[4])
        return slope - jnp.stack([diverge, diff_circ[4], push, diff_axial[4], diverge])

    def advance(s, j, slope):
        base = plane_at(0, j)
        if s == 0:
            total[j] = slope
        elif s < sections - 1:
            total[j] += BLEND[s] * slope
        else:
            out_ref[:, axial(j)] = base + (STEP_SIZE / 6.0) * (total[j] + BLEND[s] * slope)
        if s < sections - 1:
            ahead = (base + STAGE[s] * slope).reshape(rows, width)
            field[s + 1, place(j), :] = ahead
            if j == inner:
                plane_out[s + 1] = ahead

    def send_planes(s):
        for apart in reversed(range(n_circ)):
            plane_copy(s, apart).start()

    arrivals = n_circ + 2 + jnp.where(has_low, 1, 0) + jnp.where(has_high, 1, 0)
    pl.semaphore_wait(barrier, arrivals)
    send_planes(0)
    send_halos(0, 1)
    send_halos(0, 0)

    for s in range(sections):
        table[s] = build_table(index_ref[s], weight_ref[s])
        await_halos(s, 0)
        edges = [circ_in[s, 0, side] for side in range(2)]
        for j in range(inner):
            advance(s, j, slope_at(s, j, 0, edges))
        if s < sections - 1:
            send_halos(s + 1, 0)

        await_halos(s, 1)
        edges = [circ_in[s, 1, side] for side in range(2)]
        slope = slope_at(s, inner, 1, edges)
        for source in range(n_circ):
            plane_arrival(s, source).wait_recv()
        shift = jnp.where(ax == 1, offset_ref[s], n_circ - offset_ref[s])
        faced = plane_in[s][lax.rem(circ + shift, n_circ)]
        ghost = interpolate(faced, table[s]).reshape(nvar, nradial, width)
        slant = toward * ghost
        none = jnp.zeros_like(slant[0])
        slope = slope + eddy_ref[axial(inner)][None] * ghost - AXIAL_MACH * slant
        slope = slope - jnp.stack([slant[3], none, none, slant[4], slant[3]])
        advance(s, inner, slope)
        if s < sections - 1:
            send_planes(s + 1)
            send_halos(s + 1, 1)

    for s in range(sections):
        for apart in range(n_circ):
            plane_copy(s, apart).wait_send()
        for part in range(2):
            for side in range(2):
                circ_copy(s, part, side).wait_send()

                @pl.when(sends_rad[side])
                def _():
                    rad_copy(s, part, side).wait_send()


def solution(mesh):
    n_circ, n_rad = mesh.shape["circ"], mesh.shape["rad"]

    def local(state, eddy, offsets, stencil_index, stencil_weight):
        nvar, naxial, nradial, width = state.shape
        sections = offsets.shape[0]
        taps = stencil_index.shape[3]
        rows, inner = nvar * nradial, naxial - 1
        whole = pl.BlockSpec(memory_space=pltpu.HBM)
        buffer = lambda *shape: pltpu.VMEM(shape, jnp.float32)
        copies = lambda *shape: pltpu.SemaphoreType.DMA(shape)
        return pl.pallas_call(
            functools.partial(kernel, n_circ, n_rad),
            out_shape=jax.ShapeDtypeStruct(state.shape, jnp.float32),
            in_specs=[whole] * 5,
            out_specs=pl.BlockSpec(memory_space=pltpu.VMEM),
            scratch_shapes=[
                buffer(*state.shape),
                buffer(*eddy.shape),
                pltpu.SMEM((sections,), jnp.int32),
                pltpu.VMEM((sections, taps, width), jnp.int32),
                buffer(sections, taps, width),
                buffer(sections, rows * naxial, width),
                buffer(naxial, nvar, nradial, width),
                pltpu.VMEM((sections, 2 * width, 2 * width), jnp.bfloat16),
                buffer(sections, rows, width),
                buffer(sections, 2, inner * nvar, width),
                buffer(sections, 2, inner * nvar, width),
                buffer(sections, 2, nvar, width),
                buffer(sections, 2, nvar, width),
                buffer(sections, 2, 2, nradial, width),
                buffer(sections, 2, 2, nradial, width),
                copies(5),
                copies(sections, n_circ),
                copies(sections, n_circ),
                copies(sections, 2, 2),
                copies(sections, 2, 2),
                copies(sections, 2, 2),
                copies(sections, 2, 2),
                *[buffer(n_circ, rows, width) for _ in range(sections)],
            ],
            compiler_params=pltpu.CompilerParams(
                collective_id=0, has_side_effects=True, vmem_limit_bytes=60 * 1024 * 1024
            ),
        )(state, eddy, offsets, jnp.swapaxes(stencil_index, 2, 3), jnp.swapaxes(stencil_weight, 2, 3))

    return jax.shard_map(
        local,
        mesh=mesh,
        in_specs=(P(None, "ax", "rad", "circ"), P("ax", "rad", "circ"), P(), P(), P()),
        out_specs=P(None, "ax", "rad", "circ"),
        check_vma=False,
    )
```

```python
import functools

import jax
import jax.numpy as jnp
from jax import lax
from jax.experimental import pallas as pl
from jax.experimental.pallas import tpu as pltpu
from jax.sharding import PartitionSpec as P

AXIAL_MACH = 0.4
STEP_SIZE = 0.3
MESH = pl.DeviceIdType.MESH
STAGE = (0.5 * STEP_SIZE, 0.5 * STEP_SIZE, STEP_SIZE)
BLEND = (1.0, 2.0, 2.0, 1.0)


def build_table(index, weight):
    taps, width = index.shape
    normed = weight / jnp.sum(weight, axis=0, keepdims=True)
    source = lax.broadcasted_iota(jnp.int32, (width, width), 0)
    matrix = jnp.zeros((width, width), jnp.float32)
    for tap in range(taps):
        matrix += jnp.where(index[tap : tap + 1] == source, normed[tap : tap + 1], 0.0)
    high = matrix.astype(jnp.bfloat16)
    low = (matrix - high.astype(jnp.float32)).astype(jnp.bfloat16)
    top = jnp.concatenate([high, low], axis=1)
    bottom = jnp.concatenate([high, jnp.zeros_like(high)], axis=1)
    return jnp.concatenate([top, bottom], axis=0)


def interpolate(plane, table):
    width = plane.shape[1]
    high = plane.astype(jnp.bfloat16)
    low = (plane - high.astype(jnp.float32)).astype(jnp.bfloat16)
    both = jnp.dot(
        jnp.concatenate([high, low], axis=1), table, preferred_element_type=jnp.float32
    )
    return both[:, :width] + both[:, width:]


def kernel(
    n_circ, n_rad,
    state_hbm, eddy_hbm, offset_hbm, index_hbm, weight_hbm, out_ref,
    state_ref, eddy_ref, offset_ref, index_ref, weight_ref,
    field, total, table, plane_out, rad_bulk_out, rad_bulk_in, rad_front_out, rad_front_in,
    circ_out, circ_in,
    load_sem, plane_send, plane_recv, rad_send, rad_recv, circ_send, circ_recv, *plane_in,
):
    nvar, naxial, nradial, width = state_ref.shape
    sections = offset_ref.shape[0]
    rows = nvar * nradial
    inner = naxial - 1
    circ, rad, ax = lax.axis_index("circ"), lax.axis_index("rad"), lax.axis_index("ax")
    far = 1 - ax
    circ_up, circ_down = lax.rem(circ + 1, n_circ), lax.rem(circ + n_circ - 1, n_circ)
    has_low, has_high = rad > 0, rad < n_rad - 1

    loads = [
        pltpu.make_async_copy(source, target, load_sem.at[i])
        for i, (source, target) in enumerate(
            (
                (state_hbm, state_ref),
                (eddy_hbm, eddy_ref),
                (offset_hbm, offset_ref),
                (index_hbm.at[ax], index_ref),
                (weight_hbm.at[ax], weight_ref),
            )
        )
    ]
    for load in loads:
        load.start()

    barrier = pltpu.get_barrier_semaphore()

    def greet(device):
        pl.semaphore_signal(barrier, inc=1, device_id=device, device_id_type=MESH)

    for apart in range(n_circ):
        greet((lax.rem(circ + apart, n_circ), rad, far))
    greet((circ_up, rad, ax))
    greet((circ_down, rad, ax))

    @pl.when(has_low)
    def _():
        greet((circ, rad - 1, ax))

    @pl.when(has_high)
    def _():
        greet((circ, rad + 1, ax))

    for side, missing in ((0, jnp.logical_not(has_low)), (1, jnp.logical_not(has_high))):

        @pl.when(missing)
        def _():
            for s in range(sections):
                rad_bulk_in[s, side] = jnp.zeros((inner * nvar, width), jnp.float32)
                rad_front_in[s, side] = jnp.zeros((nvar, width), jnp.float32)

    def axial(j):
        return jnp.where(ax == 0, j, naxial - 1 - j)

    def place(j):
        return pl.ds(j * rows, rows)

    def plane_at(s, j):
        return field[s, place(j), :].reshape(nvar, nradial, width)

    for load in loads:
        load.wait()
    for j in range(naxial):
        field[0, place(j), :] = state_ref[:, axial(j)].reshape(rows, width)
    plane_out[0] = field[0, place(inner), :]

    def plane_copy(s, turn):
        target = jnp.where(circ < n_circ // 2, n_circ - 1 - turn, turn)
        return pltpu.make_async_remote_copy(
            src_ref=plane_out.at[s], dst_ref=plane_in[s].at[circ],
            send_sem=plane_send.at[s, turn], recv_sem=plane_recv.at[s, circ],
            device_id=(target, rad, far), device_id_type=MESH,
        )

    def plane_arrival(s, source):
        return pltpu.make_async_remote_copy(
            src_ref=plane_out.at[s], dst_ref=plane_in[s].at[source],
            send_sem=plane_send.at[s, 0], recv_sem=plane_recv.at[s, source],
            device_id=(source, rad, far), device_id_type=MESH,
        )

    def circ_copy(s, part, side):
        return pltpu.make_async_remote_copy(
            src_ref=circ_out.at[s, part, side], dst_ref=circ_in.at[s, part, side],
            send_sem=circ_send.at[s, part, side], recv_sem=circ_recv.at[s, part, side],
            device_id=(circ_up if side == 0 else circ_down, rad, ax), device_id_type=MESH,
        )

    rad_outs, rad_ins = (rad_bulk_out, rad_front_out), (rad_bulk_in, rad_front_in)

    def rad_copy(s, part, side):
        return pltpu.make_async_remote_copy(
            src_ref=rad_outs[part].at[s, side], dst_ref=rad_ins[part].at[s, side],
            send_sem=rad_send.at[s, part, side], recv_sem=rad_recv.at[s, part, side],
            device_id=(circ, rad + 1 if side == 0 else rad - 1, ax), device_id_type=MESH,
        )

    sends_rad = (has_high, has_low)
    gets_rad = (has_low, has_high)
    spans = ((0, inner), (inner, naxial))

    def send_halos(s, part):
        first, stop = spans[part]
        tiles = (stop - first) * nvar
        cells = field[s, first * rows : stop * rows, :].reshape(tiles, nradial, width)
        lane_of = lax.broadcasted_iota(jnp.int32, cells.shape, 2)
        tile_of = lax.broadcasted_iota(jnp.int32, cells.shape, 0)
        for side, edge in ((0, width - 1), (1, 0)):
            column = jnp.broadcast_to(cells[:, :, edge : edge + 1], cells.shape)
            circ_out[s, part, side] = jnp.sum(jnp.where(lane_of == tile_of, column, 0.0), axis=0)
            circ_copy(s, part, side).start()
        for side, edge in ((0, nradial - 1), (1, 0)):
            start = first * rows + edge
            rad_outs[part][s, side] = field[s, pl.ds(start, tiles, stride=nradial), :]

            @pl.when(sends_rad[side])
            def _():
                rad_copy(s, part, side).start()

    def await_halos(s, part):
        for side in range(2):
            circ_copy(s, part, side).wait_recv()

            @pl.when(gets_rad[side])
            def _():
                rad_copy(s, part, side).wait_recv()

    lane = lax.broadcasted_iota(jnp.int32, (nvar, nradial, width), 2)
    sub = lax.broadcasted_iota(jnp.int32, (nvar, nradial, width), 1)
    zero = jnp.zeros((nvar, nradial, width), jnp.float32)
    swirl = jnp.where(ax == 1, -0.3, 0.2).astype(jnp.float32)
    toward = jnp.where(ax == 1, -0.5, 0.5).astype(jnp.float32)

    def slope_at(s, j, part, edges):
        first = (j - spans[part][0]) * nvar

        def spread(side):
            return jnp.stack(
                [
                    jnp.broadcast_to(edges[side][:, t : t + 1], (nradial, width))
                    for t in range(first, first + nvar)
                ]
            )

        def spread_rows(side):
            picked = rad_ins[part][s, side, first : first + nvar, :]
            return jnp.broadcast_to(picked[:, None, :], (nvar, nradial, width))

        q = plane_at(s, j)
        before = plane_at(s, j - 1) if j > 0 else zero
        after = plane_at(s, j + 1) if j < inner else zero
        circ_low = jnp.where(lane == 0, spread(0), pltpu.roll(q, 1, 2))
        circ_high = jnp.where(lane == width - 1, spread(1), pltpu.roll(q, width - 1, 2))
        rad_low = jnp.where(sub == 0, spread_rows(0), pltpu.roll(q, 1, 1))
        rad_high = jnp.where(sub == nradial - 1, spread_rows(1), pltpu.roll(q, nradial - 1, 1))
        diff_circ = 0.5 * (circ_high - circ_low)
        diff_axial = toward * (after - before)
        laplace = (circ_high + circ_low) + (rad_high + rad_low) + (after + before) - 6.0 * q
        slope = eddy_ref[axial(j)][None] * laplace - (swirl * diff_circ + AXIAL_MACH * diff_axial)
        diverge = diff_circ[1] + 0.5 * (rad_high[2] - rad_low[2]) + diff_axial[3]
        push = 0.5 * (rad_high[4] - rad_low[4])
        return slope - jnp.stack([diverge, diff_circ[4], push, diff_axial[4], diverge])

    def advance(s, j, slope):
        base = plane_at(0, j)
        if s == 0:
            total[j] = slope
        elif s < sections - 1:
            total[j] += BLEND[s] * slope
        else:
            out_ref[:, axial(j)] = (STEP_SIZE / 6.0) * (total[j] + BLEND[s] * slope)
        if s < sections - 1:
            ahead = (base + STAGE[s] * slope).reshape(rows, width)
            field[s + 1, place(j), :] = ahead
            if j == inner:
                plane_out[s + 1] = ahead

    def send_planes(s):
        for turn in range(n_circ):
            plane_copy(s, turn).start()

    arrivals = n_circ + 2 + jnp.where(has_low, 1, 0) + jnp.where(has_high, 1, 0)
    pl.semaphore_wait(barrier, arrivals)
    send_planes(0)
    send_halos(0, 1)
    send_halos(0, 0)

    for s in range(sections):
        table[s] = build_table(index_ref[s], weight_ref[s])
        await_halos(s, 0)
        edges = [circ_in[s, 0, side] for side in range(2)]
        for j in range(inner):
            advance(s, j, slope_at(s, j, 0, edges))
        if s < sections - 1:
            send_halos(s + 1, 0)

        await_halos(s, 1)
        edges = [circ_in[s, 1, side] for side in range(2)]
        slope = slope_at(s, inner, 1, edges)
        for source in range(n_circ):
            plane_arrival(s, source).wait_recv()
        shift = jnp.where(ax == 1, offset_ref[s], n_circ - offset_ref[s])
        faced = plane_in[s][lax.rem(circ + shift, n_circ)]
        ghost = interpolate(faced, table[s]).reshape(nvar, nradial, width)
        slant = toward * ghost
        none = jnp.zeros_like(slant[0])
        slope = slope + eddy_ref[axial(inner)][None] * ghost - AXIAL_MACH * slant
        slope = slope - jnp.stack([slant[3], none, none, slant[4], slant[3]])
        advance(s, inner, slope)
        if s < sections - 1:
            send_planes(s + 1)
            send_halos(s + 1, 1)

    for s in range(sections):
        for turn in range(n_circ):
            plane_copy(s, turn).wait_send()
        for part in range(2):
            for side in range(2):
                circ_copy(s, part, side).wait_send()

                @pl.when(sends_rad[side])
                def _():
                    rad_copy(s, part, side).wait_send()


def solution(mesh):
    n_circ, n_rad = mesh.shape["circ"], mesh.shape["rad"]

    def local(state, eddy, offsets, stencil_index, stencil_weight):
        nvar, naxial, nradial, width = state.shape
        sections = offsets.shape[0]
        taps = stencil_index.shape[3]
        rows, inner = nvar * nradial, naxial - 1
        whole = pl.BlockSpec(memory_space=pltpu.HBM)
        buffer = lambda *shape: pltpu.VMEM(shape, jnp.float32)
        copies = lambda *shape: pltpu.SemaphoreType.DMA(shape)
        step = pl.pallas_call(
            functools.partial(kernel, n_circ, n_rad),
            out_shape=jax.ShapeDtypeStruct(state.shape, jnp.float32),
            in_specs=[whole] * 5,
            out_specs=pl.BlockSpec(memory_space=pltpu.VMEM),
            scratch_shapes=[
                buffer(*state.shape),
                buffer(*eddy.shape),
                pltpu.SMEM((sections,), jnp.int32),
                pltpu.VMEM((sections, taps, width), jnp.int32),
                buffer(sections, taps, width),
                buffer(sections, rows * naxial, width),
                buffer(naxial, nvar, nradial, width),
                pltpu.VMEM((sections, 2 * width, 2 * width), jnp.bfloat16),
                buffer(sections, rows, width),
                buffer(sections, 2, inner * nvar, width),
                buffer(sections, 2, inner * nvar, width),
                buffer(sections, 2, nvar, width),
                buffer(sections, 2, nvar, width),
                buffer(sections, 2, 2, nradial, width),
                buffer(sections, 2, 2, nradial, width),
                copies(5),
                copies(sections, n_circ),
                copies(sections, n_circ),
                copies(sections, 2, 2),
                copies(sections, 2, 2),
                copies(sections, 2, 2),
                copies(sections, 2, 2),
                *[buffer(n_circ, rows, width) for _ in range(sections)],
            ],
            compiler_params=pltpu.CompilerParams(
                collective_id=0, has_side_effects=True, vmem_limit_bytes=60 * 1024 * 1024
            ),
        )(state, eddy, offsets, jnp.swapaxes(stencil_index, 2, 3), jnp.swapaxes(stencil_weight, 2, 3))
        return state + step

    return jax.shard_map(
        local,
        mesh=mesh,
        in_specs=(P(None, "ax", "rad", "circ"), P("ax", "rad", "circ"), P(), P(), P()),
        out_specs=P(None, "ax", "rad", "circ"),
        check_vma=False,
    )
```

```python
import functools

import jax
import jax.numpy as jnp
from jax import lax
from jax.experimental import pallas as pl
from jax.experimental.pallas import tpu as pltpu
from jax.sharding import PartitionSpec as P

AXIAL_MACH = 0.4
STEP_SIZE = 0.3
MESH = pl.DeviceIdType.MESH
STAGE = (0.5 * STEP_SIZE, 0.5 * STEP_SIZE, STEP_SIZE)
BLEND = (1.0, 2.0, 2.0, 1.0)


def build_table(index, weight):
    taps, width = index.shape
    normed = weight / jnp.sum(weight, axis=0, keepdims=True)
    source = lax.broadcasted_iota(jnp.int32, (width, width), 0)
    matrix = jnp.zeros((width, width), jnp.float32)
    for tap in range(taps):
        matrix += jnp.where(index[tap : tap + 1] == source, normed[tap : tap + 1], 0.0)
    high = matrix.astype(jnp.bfloat16)
    low = (matrix - high.astype(jnp.float32)).astype(jnp.bfloat16)
    top = jnp.concatenate([high, low], axis=1)
    bottom = jnp.concatenate([high, jnp.zeros_like(high)], axis=1)
    return jnp.concatenate([top, bottom], axis=0)


def interpolate(plane, table):
    width = plane.shape[1]
    high = plane.astype(jnp.bfloat16)
    low = (plane - high.astype(jnp.float32)).astype(jnp.bfloat16)
    both = jnp.dot(
        jnp.concatenate([high, low], axis=1), table, preferred_element_type=jnp.float32
    )
    return both[:, :width] + both[:, width:]


def kernel(
    n_circ, n_rad,
    state_hbm, eddy_hbm, offset_hbm, index_hbm, weight_hbm, out_ref,
    state_ref, eddy_ref, offset_ref, index_ref, weight_ref,
    field, total, table, plane_out, rad_bulk_out, rad_bulk_in, rad_front_out, rad_front_in,
    circ_out, circ_in,
    load_sem, plane_send, plane_recv, rad_send, rad_recv, circ_send, circ_recv, *plane_in,
):
    nvar, naxial, nradial, width = state_ref.shape
    sections = offset_ref.shape[0]
    rows = nvar * nradial
    inner = naxial - 1
    circ, rad, ax = lax.axis_index("circ"), lax.axis_index("rad"), lax.axis_index("ax")
    far = 1 - ax
    circ_up, circ_down = lax.rem(circ + 1, n_circ), lax.rem(circ + n_circ - 1, n_circ)
    has_low, has_high = rad > 0, rad < n_rad - 1

    loads = [
        pltpu.make_async_copy(source, target, load_sem.at[i])
        for i, (source, target) in enumerate(
            (
                (state_hbm, state_ref),
                (eddy_hbm, eddy_ref),
                (offset_hbm, offset_ref),
                (index_hbm.at[ax], index_ref),
                (weight_hbm.at[ax], weight_ref),
            )
        )
    ]
    for load in loads:
        load.start()

    barrier = pltpu.get_barrier_semaphore()

    def greet(device):
        pl.semaphore_signal(barrier, inc=1, device_id=device, device_id_type=MESH)

    for apart in range(n_circ):
        greet((lax.rem(circ + apart, n_circ), rad, far))
    greet((circ_up, rad, ax))
    greet((circ_down, rad, ax))

    @pl.when(has_low)
    def _():
        greet((circ, rad - 1, ax))

    @pl.when(has_high)
    def _():
        greet((circ, rad + 1, ax))

    for side, missing in ((0, jnp.logical_not(has_low)), (1, jnp.logical_not(has_high))):

        @pl.when(missing)
        def _():
            for s in range(sections):
                rad_bulk_in[s, side] = jnp.zeros((inner * nvar, width), jnp.float32)
                rad_front_in[s, side] = jnp.zeros((nvar, width), jnp.float32)

    def axial(j):
        return jnp.where(ax == 0, j, naxial - 1 - j)

    def place(j):
        return pl.ds(j * rows, rows)

    def plane_at(s, j):
        return field[s, place(j), :].reshape(nvar, nradial, width)

    for load in loads:
        load.wait()
    for j in range(naxial):
        field[0, place(j), :] = state_ref[:, axial(j)].reshape(rows, width)
    plane_out[0] = field[0, place(inner), :]

    def plane_copy(s, turn):
        target = jnp.where(circ < n_circ // 2, n_circ - 1 - turn, turn)
        return pltpu.make_async_remote_copy(
            src_ref=plane_out.at[s], dst_ref=plane_in[s].at[circ],
            send_sem=plane_send.at[s, turn], recv_sem=plane_recv.at[s, circ],
            device_id=(target, rad, far), device_id_type=MESH,
        )

    def plane_arrival(s, source):
        return pltpu.make_async_remote_copy(
            src_ref=plane_out.at[s], dst_ref=plane_in[s].at[source],
            send_sem=plane_send.at[s, 0], recv_sem=plane_recv.at[s, source],
            device_id=(source, rad, far), device_id_type=MESH,
        )

    def circ_copy(s, part, side):
        return pltpu.make_async_remote_copy(
            src_ref=circ_out.at[s, part, side], dst_ref=circ_in.at[s, part, side],
            send_sem=circ_send.at[s, part, side], recv_sem=circ_recv.at[s, part, side],
            device_id=(circ_up if side == 0 else circ_down, rad, ax), device_id_type=MESH,
        )

    rad_outs, rad_ins = (rad_bulk_out, rad_front_out), (rad_bulk_in, rad_front_in)

    def rad_copy(s, part, side):
        return pltpu.make_async_remote_copy(
            src_ref=rad_outs[part].at[s, side], dst_ref=rad_ins[part].at[s, side],
            send_sem=rad_send.at[s, part, side], recv_sem=rad_recv.at[s, part, side],
            device_id=(circ, rad + 1 if side == 0 else rad - 1, ax), device_id_type=MESH,
        )

    sends_rad = (has_high, has_low)
    gets_rad = (has_low, has_high)
    spans = ((0, inner), (inner, naxial))

    def send_halos(s, part):
        first, stop = spans[part]
        tiles = (stop - first) * nvar
        cells = field[s, first * rows : stop * rows, :].reshape(tiles, nradial, width)
        lane_of = lax.broadcasted_iota(jnp.int32, cells.shape, 2)
        tile_of = lax.broadcasted_iota(jnp.int32, cells.shape, 0)
        for side, edge in ((0, width - 1), (1, 0)):
            column = jnp.broadcast_to(cells[:, :, edge : edge + 1], cells.shape)
            circ_out[s, part, side] = jnp.sum(jnp.where(lane_of == tile_of, column, 0.0), axis=0)
            circ_copy(s, part, side).start()
        for side, edge in ((0, nradial - 1), (1, 0)):
            start = first * rows + edge
            rad_outs[part][s, side] = field[s, pl.ds(start, tiles, stride=nradial), :]

            @pl.when(sends_rad[side])
            def _():
                rad_copy(s, part, side).start()

    def await_halos(s, part):
        for side in range(2):
            circ_copy(s, part, side).wait_recv()

            @pl.when(gets_rad[side])
            def _():
                rad_copy(s, part, side).wait_recv()

    lane = lax.broadcasted_iota(jnp.int32, (nvar, nradial, width), 2)
    sub = lax.broadcasted_iota(jnp.int32, (nvar, nradial, width), 1)
    zero = jnp.zeros((nvar, nradial, width), jnp.float32)
    swirl = jnp.where(ax == 1, -0.3, 0.2).astype(jnp.float32)
    toward = jnp.where(ax == 1, -0.5, 0.5).astype(jnp.float32)

    def slope_at(s, j, part, edges):
        first = (j - spans[part][0]) * nvar

        def spread(side):
            return jnp.stack(
                [
                    jnp.broadcast_to(edges[side][:, t : t + 1], (nradial, width))
                    for t in range(first, first + nvar)
                ]
            )

        def spread_rows(side):
            picked = rad_ins[part][s, side, first : first + nvar, :]
            return jnp.broadcast_to(picked[:, None, :], (nvar, nradial, width))

        q = plane_at(s, j)
        before = plane_at(s, j - 1) if j > 0 else zero
        after = plane_at(s, j + 1) if j < inner else zero
        circ_low = jnp.where(lane == 0, spread(0), pltpu.roll(q, 1, 2))
        circ_high = jnp.where(lane == width - 1, spread(1), pltpu.roll(q, width - 1, 2))
        rad_low = jnp.where(sub == 0, spread_rows(0), pltpu.roll(q, 1, 1))
        rad_high = jnp.where(sub == nradial - 1, spread_rows(1), pltpu.roll(q, nradial - 1, 1))
        diff_circ = 0.5 * (circ_high - circ_low)
        diff_axial = toward * (after - before)
        laplace = (circ_high + circ_low) + (rad_high + rad_low) + (after + before) - 6.0 * q
        slope = eddy_ref[axial(j)][None] * laplace - (swirl * diff_circ + AXIAL_MACH * diff_axial)
        diverge = diff_circ[1] + 0.5 * (rad_high[2] - rad_low[2]) + diff_axial[3]
        push = 0.5 * (rad_high[4] - rad_low[4])
        return slope - jnp.stack([diverge, diff_circ[4], push, diff_axial[4], diverge])

    def advance(s, j, slope):
        base = plane_at(0, j)
        if s == 0:
            total[j] = slope
        elif s < sections - 1:
            total[j] += BLEND[s] * slope
        else:
            out_ref[:, axial(j)] = base + (STEP_SIZE / 6.0) * (total[j] + BLEND[s] * slope)
        if s < sections - 1:
            ahead = (base + STAGE[s] * slope).reshape(rows, width)
            field[s + 1, place(j), :] = ahead
            if j == inner:
                plane_out[s + 1] = ahead

    def send_planes(s):
        for turn in range(n_circ):
            plane_copy(s, turn).start()

    arrivals = n_circ + 2 + jnp.where(has_low, 1, 0) + jnp.where(has_high, 1, 0)
    pl.semaphore_wait(barrier, arrivals)
    send_planes(0)
    send_halos(0, 1)
    send_halos(0, 0)

    for s in range(sections):
        table[s] = build_table(index_ref[s], weight_ref[s])
        await_halos(s, 0)
        edges = [circ_in[s, 0, side] for side in range(2)]
        for j in range(inner):
            advance(s, j, slope_at(s, j, 0, edges))
        if s < sections - 1:
            send_halos(s + 1, 0)

        await_halos(s, 1)
        edges = [circ_in[s, 1, side] for side in range(2)]
        slope = slope_at(s, inner, 1, edges)
        for source in range(n_circ):
            plane_arrival(s, source).wait_recv()
        shift = jnp.where(ax == 1, offset_ref[s], n_circ - offset_ref[s])
        faced = plane_in[s][lax.rem(circ + shift, n_circ)]
        ghost = interpolate(faced, table[s]).reshape(nvar, nradial, width)
        slant = toward * ghost
        none = jnp.zeros_like(slant[0])
        slope = slope + eddy_ref[axial(inner)][None] * ghost - AXIAL_MACH * slant
        slope = slope - jnp.stack([slant[3], none, none, slant[4], slant[3]])
        advance(s, inner, slope)
        if s < sections - 1:
            send_planes(s + 1)
            send_halos(s + 1, 1)

    for s in range(sections):
        for turn in range(n_circ):
            plane_copy(s, turn).wait_send()
        for part in range(2):
            for side in range(2):
                circ_copy(s, part, side).wait_send()

                @pl.when(sends_rad[side])
                def _():
                    rad_copy(s, part, side).wait_send()


def solution(mesh):
    n_circ, n_rad = mesh.shape["circ"], mesh.shape["rad"]

    def local(state, eddy, offsets, stencil_index, stencil_weight):
        nvar, naxial, nradial, width = state.shape
        sections = offsets.shape[0]
        taps = stencil_index.shape[3]
        rows, inner = nvar * nradial, naxial - 1
        whole = pl.BlockSpec(memory_space=pltpu.HBM)
        buffer = lambda *shape: pltpu.VMEM(shape, jnp.float32)
        copies = lambda *shape: pltpu.SemaphoreType.DMA(shape)
        step = pl.pallas_call(
            functools.partial(kernel, n_circ, n_rad),
            out_shape=pltpu.VMEM(state.shape, jnp.float32),
            in_specs=[whole] * 5,
            out_specs=pl.BlockSpec(memory_space=pltpu.VMEM),
            scratch_shapes=[
                buffer(*state.shape),
                buffer(*eddy.shape),
                pltpu.SMEM((sections,), jnp.int32),
                pltpu.VMEM((sections, taps, width), jnp.int32),
                buffer(sections, taps, width),
                buffer(sections, rows * naxial, width),
                buffer(naxial, nvar, nradial, width),
                pltpu.VMEM((sections, 2 * width, 2 * width), jnp.bfloat16),
                buffer(sections, rows, width),
                buffer(sections, 2, inner * nvar, width),
                buffer(sections, 2, inner * nvar, width),
                buffer(sections, 2, nvar, width),
                buffer(sections, 2, nvar, width),
                buffer(sections, 2, 2, nradial, width),
                buffer(sections, 2, 2, nradial, width),
                copies(5),
                copies(sections, n_circ),
                copies(sections, n_circ),
                copies(sections, 2, 2),
                copies(sections, 2, 2),
                copies(sections, 2, 2),
                copies(sections, 2, 2),
                *[buffer(n_circ, rows, width) for _ in range(sections)],
            ],
            compiler_params=pltpu.CompilerParams(
                collective_id=0, has_side_effects=True, vmem_limit_bytes=60 * 1024 * 1024
            ),
        )(state, eddy, offsets, jnp.swapaxes(stencil_index, 2, 3), jnp.swapaxes(stencil_weight, 2, 3))
        return step

    return jax.shard_map(
        local,
        mesh=mesh,
        in_specs=(P(None, "ax", "rad", "circ"), P("ax", "rad", "circ"), P(), P(), P()),
        out_specs=P(None, "ax", "rad", "circ"),
        check_vma=False,
    )
```

```python
import functools

import jax
import jax.numpy as jnp
from jax import lax
from jax.experimental import pallas as pl
from jax.experimental.pallas import tpu as pltpu
from jax.sharding import PartitionSpec as P

AXIAL_MACH = 0.4
STEP_SIZE = 0.3
MESH = pl.DeviceIdType.MESH
STAGE = (0.5 * STEP_SIZE, 0.5 * STEP_SIZE, STEP_SIZE)
BLEND = (1.0, 2.0, 2.0, 1.0)


def build_table(index, weight):
    taps, width = index.shape
    normed = weight / jnp.sum(weight, axis=0, keepdims=True)
    source = lax.broadcasted_iota(jnp.int32, (width, width), 0)
    matrix = jnp.zeros((width, width), jnp.float32)
    for tap in range(taps):
        matrix += jnp.where(index[tap : tap + 1] == source, normed[tap : tap + 1], 0.0)
    high = matrix.astype(jnp.bfloat16)
    low = (matrix - high.astype(jnp.float32)).astype(jnp.bfloat16)
    top = jnp.concatenate([high, low], axis=1)
    bottom = jnp.concatenate([high, jnp.zeros_like(high)], axis=1)
    return jnp.concatenate([top, bottom], axis=0)


def interpolate(plane, table):
    width = plane.shape[1]
    high = plane.astype(jnp.bfloat16)
    low = (plane - high.astype(jnp.float32)).astype(jnp.bfloat16)
    both = jnp.dot(
        jnp.concatenate([high, low], axis=1), table, preferred_element_type=jnp.float32
    )
    return both[:, :width] + both[:, width:]


def kernel(
    n_circ, n_rad,
    state_hbm, eddy_hbm, offset_hbm, index_hbm, weight_hbm, out_ref,
    state_ref, eddy_ref, offset_ref, index_ref, weight_ref,
    field, slopes, total, table, plane_out, rad_bulk_out, rad_bulk_in, rad_front_out, rad_front_in,
    circ_out, circ_in,
    load_sem, plane_send, plane_recv, rad_send, rad_recv, circ_send, circ_recv, *plane_in,
):
    nvar, naxial, nradial, width = state_ref.shape
    sections = offset_ref.shape[0]
    rows = nvar * nradial
    inner = naxial - 1
    circ, rad, ax = lax.axis_index("circ"), lax.axis_index("rad"), lax.axis_index("ax")
    far = 1 - ax
    circ_up, circ_down = lax.rem(circ + 1, n_circ), lax.rem(circ + n_circ - 1, n_circ)
    has_low, has_high = rad > 0, rad < n_rad - 1

    barrier = pltpu.get_barrier_semaphore()

    def greet(device):
        pl.semaphore_signal(barrier, inc=1, device_id=device, device_id_type=MESH)

    for apart in range(n_circ):
        greet((lax.rem(circ + apart, n_circ), rad, far))
    greet((circ_up, rad, ax))
    greet((circ_down, rad, ax))

    @pl.when(has_low)
    def _():
        greet((circ, rad - 1, ax))

    @pl.when(has_high)
    def _():
        greet((circ, rad + 1, ax))

    loads = [
        pltpu.make_async_copy(source, target, load_sem.at[i])
        for i, (source, target) in enumerate(
            (
                (state_hbm, state_ref),
                (eddy_hbm, eddy_ref),
                (offset_hbm, offset_ref),
                (index_hbm.at[ax], index_ref),
                (weight_hbm.at[ax], weight_ref),
            )
        )
    ]
    for load in loads:
        load.start()

    for side, missing in ((0, jnp.logical_not(has_low)), (1, jnp.logical_not(has_high))):

        @pl.when(missing)
        def _():
            for s in range(sections):
                rad_bulk_in[s, side] = jnp.zeros((inner * nvar, width), jnp.float32)
                rad_front_in[s, side] = jnp.zeros((nvar, width), jnp.float32)

    def axial(j):
        return jnp.where(ax == 0, j, naxial - 1 - j)

    def place(j):
        return pl.ds(j * rows, rows)

    def plane_at(s, j):
        return field[s, place(j), :].reshape(nvar, nradial, width)

    for load in loads:
        load.wait()
    for j in range(naxial):
        field[0, place(j), :] = state_ref[:, axial(j)].reshape(rows, width)
    plane_out[0] = field[0, place(inner), :]

    def plane_copy(s, turn):
        target = jnp.where(circ < n_circ // 2, n_circ - 1 - turn, turn)
        return pltpu.make_async_remote_copy(
            src_ref=plane_out.at[s], dst_ref=plane_in[s].at[circ],
            send_sem=plane_send.at[s, turn], recv_sem=plane_recv.at[s, circ],
            device_id=(target, rad, far), device_id_type=MESH,
        )

    def plane_arrival(s, source):
        return pltpu.make_async_remote_copy(
            src_ref=plane_out.at[s], dst_ref=plane_in[s].at[source],
            send_sem=plane_send.at[s, 0], recv_sem=plane_recv.at[s, source],
            device_id=(source, rad, far), device_id_type=MESH,
        )

    def circ_copy(s, part, side):
        return pltpu.make_async_remote_copy(
            src_ref=circ_out.at[s, part, side], dst_ref=circ_in.at[s, part, side],
            send_sem=circ_send.at[s, part, side], recv_sem=circ_recv.at[s, part, side],
            device_id=(circ_up if side == 0 else circ_down, rad, ax), device_id_type=MESH,
        )

    rad_outs, rad_ins = (rad_bulk_out, rad_front_out), (rad_bulk_in, rad_front_in)

    def rad_copy(s, part, side):
        return pltpu.make_async_remote_copy(
            src_ref=rad_outs[part].at[s, side], dst_ref=rad_ins[part].at[s, side],
            send_sem=rad_send.at[s, part, side], recv_sem=rad_recv.at[s, part, side],
            device_id=(circ, rad + 1 if side == 0 else rad - 1, ax), device_id_type=MESH,
        )

    sends_rad = (has_high, has_low)
    gets_rad = (has_low, has_high)
    spans = ((0, inner), (inner, naxial))

    def send_halos(s, part):
        first, stop = spans[part]
        tiles = (stop - first) * nvar
        cells = field[s, first * rows : stop * rows, :].reshape(tiles, nradial, width)
        lane_of = lax.broadcasted_iota(jnp.int32, cells.shape, 2)
        tile_of = lax.broadcasted_iota(jnp.int32, cells.shape, 0)
        for side, edge in ((0, width - 1), (1, 0)):
            column = jnp.broadcast_to(cells[:, :, edge : edge + 1], cells.shape)
            circ_out[s, part, side] = jnp.sum(jnp.where(lane_of == tile_of, column, 0.0), axis=0)
            circ_copy(s, part, side).start()
        for side, edge in ((0, nradial - 1), (1, 0)):
            start = first * rows + edge
            rad_outs[part][s, side] = field[s, pl.ds(start, tiles, stride=nradial), :]

            @pl.when(sends_rad[side])
            def _():
                rad_copy(s, part, side).start()

    def await_halos(s, part):
        for side in range(2):
            circ_copy(s, part, side).wait_recv()

            @pl.when(gets_rad[side])
            def _():
                rad_copy(s, part, side).wait_recv()

    lane = lax.broadcasted_iota(jnp.int32, (nvar, nradial, width), 2)
    sub = lax.broadcasted_iota(jnp.int32, (nvar, nradial, width), 1)
    zero = jnp.zeros((nvar, nradial, width), jnp.float32)
    swirl = jnp.where(ax == 1, -0.3, 0.2).astype(jnp.float32)
    toward = jnp.where(ax == 1, -0.5, 0.5).astype(jnp.float32)

    at_low, at_high = lane[0] == 0, lane[0] == width - 1
    at_under, at_over = sub[0] == 0, sub[0] == nradial - 1
    half = lambda where: jnp.where(where, 0.5, 0.0).astype(jnp.float32)
    half_low, half_high, half_under, half_over = map(half, (at_low, at_high, at_under, at_over))

    def inside(s, j):
        q = plane_at(s, j)
        before = plane_at(s, j - 1) if j > 0 else zero
        after = plane_at(s, j + 1) if j < inner else zero
        circ_low = jnp.where(lane == 0, 0.0, pltpu.roll(q, 1, 2))
        circ_high = jnp.where(lane == width - 1, 0.0, pltpu.roll(q, width - 1, 2))
        rad_low = jnp.where(sub == 0, 0.0, pltpu.roll(q, 1, 1))
        rad_high = jnp.where(sub == nradial - 1, 0.0, pltpu.roll(q, nradial - 1, 1))
        diff_circ = 0.5 * (circ_high - circ_low)
        diff_axial = toward * (after - before)
        laplace = (circ_high + circ_low) + (rad_high + rad_low) + (after + before) - 6.0 * q
        slope = eddy_ref[axial(j)][None] * laplace - (swirl * diff_circ + AXIAL_MACH * diff_axial)
        diverge = diff_circ[1] + 0.5 * (rad_high[2] - rad_low[2]) + diff_axial[3]
        push = 0.5 * (rad_high[4] - rad_low[4])
        return slope - jnp.stack([diverge, diff_circ[4], push, diff_axial[4], diverge])

    def from_halos(s, j, part, edges):
        first = (j - spans[part][0]) * nvar
        eddy = eddy_ref[axial(j)]
        by_low = jnp.where(at_low, eddy + 0.5 * swirl, 0.0)
        by_high = jnp.where(at_high, eddy - 0.5 * swirl, 0.0)
        by_under = jnp.where(at_under, eddy, 0.0)
        by_over = jnp.where(at_over, eddy, 0.0)

        def column(side, v):
            t = first + v
            return jnp.broadcast_to(edges[side][:, t : t + 1], (nradial, width))

        def row(side, v):
            picked = rad_ins[part][s, side, first + v : first + v + 1, :]
            return jnp.broadcast_to(picked, (nradial, width))

        low, high = ([column(side, v) for v in range(nvar)] for side in range(2))
        under, over = ([row(side, v) for v in range(nvar)] for side in range(2))
        added = [
            (by_low * low[v] + by_high * high[v]) + (by_under * under[v] + by_over * over[v])
            for v in range(nvar)
        ]
        spread = (half_low * low[1] - half_high * high[1]) + (
            half_under * under[2] - half_over * over[2]
        )
        added[0] += spread
        added[1] += half_low * low[4] - half_high * high[4]
        added[2] += half_under * under[4] - half_over * over[4]
        added[4] += spread
        return jnp.stack(added)

    def advance(s, j, slope):
        base = plane_at(0, j)
        if s == 0:
            total[j] = slope
        elif s < sections - 1:
            total[j] += BLEND[s] * slope
        else:
            out_ref[:, axial(j)] = base + (STEP_SIZE / 6.0) * (total[j] + BLEND[s] * slope)
        if s < sections - 1:
            ahead = (base + STAGE[s] * slope).reshape(rows, width)
            field[s + 1, place(j), :] = ahead
            if j == inner:
                plane_out[s + 1] = ahead

    def send_planes(s):
        for turn in range(n_circ):
            plane_copy(s, turn).start()

    arrivals = n_circ + 2 + jnp.where(has_low, 1, 0) + jnp.where(has_high, 1, 0)
    pl.semaphore_wait(barrier, arrivals)
    send_planes(0)
    send_halos(0, 1)
    send_halos(0, 0)

    for s in range(sections):
        table[s] = build_table(index_ref[s], weight_ref[s])
        for j in range(naxial):
            slopes[j] = inside(s, j)
        await_halos(s, 0)
        edges = [circ_in[s, 0, side] for side in range(2)]
        for j in range(inner):
            advance(s, j, slopes[j] + from_halos(s, j, 0, edges))
        if s < sections - 1:
            send_halos(s + 1, 0)

        await_halos(s, 1)
        edges = [circ_in[s, 1, side] for side in range(2)]
        slope = slopes[inner] + from_halos(s, inner, 1, edges)
        for source in range(n_circ):
            plane_arrival(s, source).wait_recv()
        shift = jnp.where(ax == 1, offset_ref[s], n_circ - offset_ref[s])
        faced = plane_in[s][lax.rem(circ + shift, n_circ)]
        ghost = interpolate(faced, table[s]).reshape(nvar, nradial, width)
        slant = toward * ghost
        none = jnp.zeros_like(slant[0])
        slope = slope + eddy_ref[axial(inner)][None] * ghost - AXIAL_MACH * slant
        slope = slope - jnp.stack([slant[3], none, none, slant[4], slant[3]])
        advance(s, inner, slope)
        if s < sections - 1:
            send_planes(s + 1)
            send_halos(s + 1, 1)

    for s in range(sections):
        for turn in range(n_circ):
            plane_copy(s, turn).wait_send()
        for part in range(2):
            for side in range(2):
                circ_copy(s, part, side).wait_send()

                @pl.when(sends_rad[side])
                def _():
                    rad_copy(s, part, side).wait_send()


def solution(mesh):
    n_circ, n_rad = mesh.shape["circ"], mesh.shape["rad"]

    def local(state, eddy, offsets, stencil_index, stencil_weight):
        nvar, naxial, nradial, width = state.shape
        sections = offsets.shape[0]
        taps = stencil_index.shape[3]
        rows, inner = nvar * nradial, naxial - 1
        whole = pl.BlockSpec(memory_space=pltpu.HBM)
        buffer = lambda *shape: pltpu.VMEM(shape, jnp.float32)
        copies = lambda *shape: pltpu.SemaphoreType.DMA(shape)
        step = pl.pallas_call(
            functools.partial(kernel, n_circ, n_rad),
            out_shape=pltpu.VMEM(state.shape, jnp.float32),
            in_specs=[whole] * 5,
            out_specs=pl.BlockSpec(memory_space=pltpu.VMEM),
            scratch_shapes=[
                buffer(*state.shape),
                buffer(*eddy.shape),
                pltpu.SMEM((sections,), jnp.int32),
                pltpu.VMEM((sections, taps, width), jnp.int32),
                buffer(sections, taps, width),
                buffer(sections, rows * naxial, width),
                buffer(naxial, nvar, nradial, width),
                buffer(naxial, nvar, nradial, width),
                pltpu.VMEM((sections, 2 * width, 2 * width), jnp.bfloat16),
                buffer(sections, rows, width),
                buffer(sections, 2, inner * nvar, width),
                buffer(sections, 2, inner * nvar, width),
                buffer(sections, 2, nvar, width),
                buffer(sections, 2, nvar, width),
                buffer(sections, 2, 2, nradial, width),
                buffer(sections, 2, 2, nradial, width),
                copies(5),
                copies(sections, n_circ),
                copies(sections, n_circ),
                copies(sections, 2, 2),
                copies(sections, 2, 2),
                copies(sections, 2, 2),
                copies(sections, 2, 2),
                *[buffer(n_circ, rows, width) for _ in range(sections)],
            ],
            compiler_params=pltpu.CompilerParams(
                collective_id=0, has_side_effects=True, vmem_limit_bytes=60 * 1024 * 1024
            ),
        )(state, eddy, offsets, jnp.swapaxes(stencil_index, 2, 3), jnp.swapaxes(stencil_weight, 2, 3))
        return step

    return jax.shard_map(
        local,
        mesh=mesh,
        in_specs=(P(None, "ax", "rad", "circ"), P("ax", "rad", "circ"), P(), P(), P()),
        out_specs=P(None, "ax", "rad", "circ"),
        check_vma=False,
    )
```

```python
import functools

import jax
import jax.numpy as jnp
from jax import lax
from jax.experimental import pallas as pl
from jax.experimental.pallas import tpu as pltpu
from jax.sharding import PartitionSpec as P

AXIAL_MACH = 0.4
STEP_SIZE = 0.3
MESH = pl.DeviceIdType.MESH


def build_table(index, weight):
    taps, width = index.shape
    normed = weight / jnp.sum(weight, axis=0, keepdims=True)
    source = lax.broadcasted_iota(jnp.int32, (width, width), 0)
    matrix = jnp.zeros((width, width), jnp.float32)
    for tap in range(taps):
        matrix += jnp.where(index[tap : tap + 1] == source, normed[tap : tap + 1], 0.0)
    high = matrix.astype(jnp.bfloat16)
    low = (matrix - high.astype(jnp.float32)).astype(jnp.bfloat16)
    top = jnp.concatenate([high, low], axis=1)
    bottom = jnp.concatenate([high, jnp.zeros_like(high)], axis=1)
    return jnp.concatenate([top, bottom], axis=0)


def interpolate(plane, table):
    width = plane.shape[1]
    high = plane.astype(jnp.bfloat16)
    low = (plane - high.astype(jnp.float32)).astype(jnp.bfloat16)
    both = jnp.dot(
        jnp.concatenate([high, low], axis=1), table, preferred_element_type=jnp.float32
    )
    return both[:, :width] + both[:, width:]


def kernel(
    n_circ, n_rad,
    state_hbm, eddy_hbm, offset_hbm, index_hbm, weight_hbm, out_ref,
    state_ref, eddy_ref, offset_ref, index_ref, weight_ref,
    field, slopes, total, table, plane_out, rad_bulk_out, rad_bulk_in, rad_front_out, rad_front_in,
    circ_out, circ_in,
    load_sem, plane_send, plane_recv, rad_send, rad_recv, circ_send, circ_recv, plane_in,
):
    nvar, naxial, nradial, width = state_ref.shape
    sections = offset_ref.shape[0]
    rows = nvar * nradial
    inner = naxial - 1
    circ, rad, ax = lax.axis_index("circ"), lax.axis_index("rad"), lax.axis_index("ax")
    far = 1 - ax
    circ_up, circ_down = lax.rem(circ + 1, n_circ), lax.rem(circ + n_circ - 1, n_circ)
    has_low, has_high = rad > 0, rad < n_rad - 1

    barrier = pltpu.get_barrier_semaphore()

    def greet(device):
        pl.semaphore_signal(barrier, inc=1, device_id=device, device_id_type=MESH)

    for apart in range(n_circ):
        greet((lax.rem(circ + apart, n_circ), rad, far))
    greet((circ_up, rad, ax))
    greet((circ_down, rad, ax))

    @pl.when(has_low)
    def _():
        greet((circ, rad - 1, ax))

    @pl.when(has_high)
    def _():
        greet((circ, rad + 1, ax))

    loads = [
        pltpu.make_async_copy(source, target, load_sem.at[i])
        for i, (source, target) in enumerate(
            (
                (state_hbm, state_ref),
                (eddy_hbm, eddy_ref),
                (offset_hbm, offset_ref),
                (index_hbm.at[ax], index_ref),
                (weight_hbm.at[ax], weight_ref),
            )
        )
    ]
    for load in loads:
        load.start()

    for side, missing in ((0, jnp.logical_not(has_low)), (1, jnp.logical_not(has_high))):

        @pl.when(missing)
        def _():
            for s in range(sections):
                rad_bulk_in[s, side] = jnp.zeros((inner * nvar, width), jnp.float32)
                rad_front_in[s, side] = jnp.zeros((nvar, width), jnp.float32)

    def axial(j):
        return jnp.where(ax == 0, j, naxial - 1 - j)

    def place(j):
        return pl.ds(j * rows, rows)

    def plane_at(s, j):
        return field[s, place(j), :].reshape(nvar, nradial, width)

    for load in loads:
        load.wait()
    for j in range(naxial):
        field[0, place(j), :] = state_ref[:, axial(j)].reshape(rows, width)
    plane_out[0] = field[0, place(inner), :]

    def plane_copy(s, turn):
        target = jnp.where(circ < n_circ // 2, n_circ - 1 - turn, turn)
        return pltpu.make_async_remote_copy(
            src_ref=plane_out.at[s], dst_ref=plane_in.at[s, circ],
            send_sem=plane_send.at[s, turn], recv_sem=plane_recv.at[s, circ],
            device_id=(target, rad, far), device_id_type=MESH,
        )

    def plane_arrival(s, source):
        return pltpu.make_async_remote_copy(
            src_ref=plane_out.at[s], dst_ref=plane_in.at[s, source],
            send_sem=plane_send.at[s, 0], recv_sem=plane_recv.at[s, source],
            device_id=(source, rad, far), device_id_type=MESH,
        )

    def circ_copy(s, part, side):
        return pltpu.make_async_remote_copy(
            src_ref=circ_out.at[s, part, side], dst_ref=circ_in.at[s, part, side],
            send_sem=circ_send.at[s, part, side], recv_sem=circ_recv.at[s, part, side],
            device_id=(circ_up if side == 0 else circ_down, rad, ax), device_id_type=MESH,
        )

    rad_outs, rad_ins = (rad_bulk_out, rad_front_out), (rad_bulk_in, rad_front_in)

    def rad_copy(s, part, side):
        return pltpu.make_async_remote_copy(
            src_ref=rad_outs[part].at[s, side], dst_ref=rad_ins[part].at[s, side],
            send_sem=rad_send.at[s, part, side], recv_sem=rad_recv.at[s, part, side],
            device_id=(circ, rad + 1 if side == 0 else rad - 1, ax), device_id_type=MESH,
        )

    sends_rad = (has_high, has_low)
    gets_rad = (has_low, has_high)
    spans = ((0, inner), (inner, naxial))

    def send_halos(s, part):
        first, stop = spans[part]
        tiles = (stop - first) * nvar
        cells = field[s, first * rows : stop * rows, :].reshape(tiles, nradial, width)
        lane_of = lax.broadcasted_iota(jnp.int32, cells.shape, 2)
        tile_of = lax.broadcasted_iota(jnp.int32, cells.shape, 0)
        for side, edge in ((0, width - 1), (1, 0)):
            column = jnp.broadcast_to(cells[:, :, edge : edge + 1], cells.shape)
            circ_out[s, part, side] = jnp.sum(jnp.where(lane_of == tile_of, column, 0.0), axis=0)
            circ_copy(s, part, side).start()
        for side, edge in ((0, nradial - 1), (1, 0)):
            start = first * rows + edge
            rad_outs[part][s, side] = field[s, pl.ds(start, tiles, stride=nradial), :]

            @pl.when(sends_rad[side])
            def _():
                rad_copy(s, part, side).start()

    def await_halos(s, part):
        for side in range(2):
            circ_copy(s, part, side).wait_recv()

            @pl.when(gets_rad[side])
            def _():
                rad_copy(s, part, side).wait_recv()

    lane = lax.broadcasted_iota(jnp.int32, (nvar, nradial, width), 2)
    sub = lax.broadcasted_iota(jnp.int32, (nvar, nradial, width), 1)
    zero = jnp.zeros((nvar, nradial, width), jnp.float32)
    swirl = jnp.where(ax == 1, -0.3, 0.2).astype(jnp.float32)
    toward = jnp.where(ax == 1, -0.5, 0.5).astype(jnp.float32)

    at_low, at_high = lane[0] == 0, lane[0] == width - 1
    at_under, at_over = sub[0] == 0, sub[0] == nradial - 1
    half = lambda where: jnp.where(where, 0.5, 0.0).astype(jnp.float32)
    half_low, half_high, half_under, half_over = map(half, (at_low, at_high, at_under, at_over))

    def inside(s, j):
        q = plane_at(s, j)
        before = plane_at(s, j - 1) if j > 0 else zero
        after = plane_at(s, j + 1) if j < inner else zero
        circ_low = jnp.where(lane == 0, 0.0, pltpu.roll(q, 1, 2))
        circ_high = jnp.where(lane == width - 1, 0.0, pltpu.roll(q, width - 1, 2))
        rad_low = jnp.where(sub == 0, 0.0, pltpu.roll(q, 1, 1))
        rad_high = jnp.where(sub == nradial - 1, 0.0, pltpu.roll(q, nradial - 1, 1))
        diff_circ = 0.5 * (circ_high - circ_low)
        diff_axial = toward * (after - before)
        laplace = (circ_high + circ_low) + (rad_high + rad_low) + (after + before) - 6.0 * q
        slope = eddy_ref[axial(j)][None] * laplace - (swirl * diff_circ + AXIAL_MACH * diff_axial)
        diverge = diff_circ[1] + 0.5 * (rad_high[2] - rad_low[2]) + diff_axial[3]
        push = 0.5 * (rad_high[4] - rad_low[4])
        return slope - jnp.stack([diverge, diff_circ[4], push, diff_axial[4], diverge])

    def from_halos(s, j, part, edges):
        first = (j - spans[part][0]) * nvar
        eddy = eddy_ref[axial(j)]
        by_low = jnp.where(at_low, eddy + 0.5 * swirl, 0.0)
        by_high = jnp.where(at_high, eddy - 0.5 * swirl, 0.0)
        by_under = jnp.where(at_under, eddy, 0.0)
        by_over = jnp.where(at_over, eddy, 0.0)

        def column(side, v):
            t = first + v
            return jnp.broadcast_to(edges[side][:, t : t + 1], (nradial, width))

        def row(side, v):
            picked = rad_ins[part][s, side, first + v : first + v + 1, :]
            return jnp.broadcast_to(picked, (nradial, width))

        low, high = ([column(side, v) for v in range(nvar)] for side in range(2))
        under, over = ([row(side, v) for v in range(nvar)] for side in range(2))
        added = [
            (by_low * low[v] + by_high * high[v]) + (by_under * under[v] + by_over * over[v])
            for v in range(nvar)
        ]
        spread = (half_low * low[1] - half_high * high[1]) + (
            half_under * under[2] - half_over * over[2]
        )
        added[0] += spread
        added[1] += half_low * low[4] - half_high * high[4]
        added[2] += half_under * under[4] - half_over * over[4]
        added[4] += spread
        return jnp.stack(added)

    def advance(s, j, slope):
        blend = jnp.where((s == 0) | (s == sections - 1), 1.0, 2.0).astype(jnp.float32)
        reach = jnp.where(s < sections - 2, 0.5 * STEP_SIZE, STEP_SIZE).astype(jnp.float32)
        total[j] += blend * slope
        ahead = (plane_at(0, j) + reach * slope).reshape(rows, width)
        field[s + 1, place(j), :] = ahead
        if j == inner:
            plane_out[s + 1] = ahead

    def send_planes(s):
        for turn in range(n_circ):
            plane_copy(s, turn).start()

    arrivals = n_circ + 2 + jnp.where(has_low, 1, 0) + jnp.where(has_high, 1, 0)
    pl.semaphore_wait(barrier, arrivals)
    send_planes(0)
    send_halos(0, 1)
    send_halos(0, 0)

    def section(s, carry):
        table[s] = build_table(index_ref[s], weight_ref[s])
        for j in range(naxial):
            slopes[j] = inside(s, j)
        await_halos(s, 0)
        edges = [circ_in[s, 0, side] for side in range(2)]
        for j in range(inner):
            advance(s, j, slopes[j] + from_halos(s, j, 0, edges))

        @pl.when(s < sections - 1)
        def _():
            send_halos(s + 1, 0)

        await_halos(s, 1)
        edges = [circ_in[s, 1, side] for side in range(2)]
        slope = slopes[inner] + from_halos(s, inner, 1, edges)
        for source in range(n_circ):
            plane_arrival(s, source).wait_recv()
        shift = jnp.where(ax == 1, offset_ref[s], n_circ - offset_ref[s])
        facing = lax.rem(circ + shift, n_circ)
        faced = plane_in[s, 0]
        for source in range(1, n_circ):
            faced = jnp.where(facing == source, plane_in[s, source], faced)
        ghost = interpolate(faced, table[s]).reshape(nvar, nradial, width)
        slant = toward * ghost
        none = jnp.zeros_like(slant[0])
        slope = slope + eddy_ref[axial(inner)][None] * ghost - AXIAL_MACH * slant
        slope = slope - jnp.stack([slant[3], none, none, slant[4], slant[3]])
        advance(s, inner, slope)

        @pl.when(s < sections - 1)
        def _():
            send_planes(s + 1)
            send_halos(s + 1, 1)

        return carry

    total[...] = jnp.zeros_like(total)
    lax.fori_loop(0, sections, section, 0)

    for j in range(naxial):
        out_ref[:, axial(j)] = plane_at(0, j) + (STEP_SIZE / 6.0) * total[j]

    def finish(s, carry):
        for turn in range(n_circ):
            plane_copy(s, turn).wait_send()
        for part in range(2):
            for side in range(2):
                circ_copy(s, part, side).wait_send()

                @pl.when(sends_rad[side])
                def _():
                    rad_copy(s, part, side).wait_send()

        return carry

    lax.fori_loop(0, sections, finish, 0)


def solution(mesh):
    n_circ, n_rad = mesh.shape["circ"], mesh.shape["rad"]

    def local(state, eddy, offsets, stencil_index, stencil_weight):
        nvar, naxial, nradial, width = state.shape
        sections = offsets.shape[0]
        taps = stencil_index.shape[3]
        rows, inner = nvar * nradial, naxial - 1
        whole = pl.BlockSpec(memory_space=pltpu.HBM)
        buffer = lambda *shape: pltpu.VMEM(shape, jnp.float32)
        copies = lambda *shape: pltpu.SemaphoreType.DMA(shape)
        step = pl.pallas_call(
            functools.partial(kernel, n_circ, n_rad),
            out_shape=pltpu.VMEM(state.shape, jnp.float32),
            in_specs=[whole] * 5,
            out_specs=pl.BlockSpec(memory_space=pltpu.VMEM),
            scratch_shapes=[
                buffer(*state.shape),
                buffer(*eddy.shape),
                pltpu.SMEM((sections,), jnp.int32),
                pltpu.VMEM((sections, taps, width), jnp.int32),
                buffer(sections, taps, width),
                buffer(sections + 1, rows * naxial, width),
                buffer(naxial, nvar, nradial, width),
                buffer(naxial, nvar, nradial, width),
                pltpu.VMEM((sections, 2 * width, 2 * width), jnp.bfloat16),
                buffer(sections + 1, rows, width),
                buffer(sections, 2, inner * nvar, width),
                buffer(sections, 2, inner * nvar, width),
                buffer(sections, 2, nvar, width),
                buffer(sections, 2, nvar, width),
                buffer(sections, 2, 2, nradial, width),
                buffer(sections, 2, 2, nradial, width),
                copies(5),
                copies(sections, n_circ),
                copies(sections, n_circ),
                copies(sections, 2, 2),
                copies(sections, 2, 2),
                copies(sections, 2, 2),
                copies(sections, 2, 2),
                buffer(sections, n_circ, rows, width),
            ],
            compiler_params=pltpu.CompilerParams(
                collective_id=0, has_side_effects=True, vmem_limit_bytes=60 * 1024 * 1024
            ),
        )(state, eddy, offsets, jnp.swapaxes(stencil_index, 2, 3), jnp.swapaxes(stencil_weight, 2, 3))
        return step

    return jax.shard_map(
        local,
        mesh=mesh,
        in_specs=(P(None, "ax", "rad", "circ"), P("ax", "rad", "circ"), P(), P(), P()),
        out_specs=P(None, "ax", "rad", "circ"),
        check_vma=False,
    )
```

```python
import functools
import itertools

import jax
import jax.numpy as jnp
from jax import lax
from jax.experimental import pallas as pl
from jax.experimental.pallas import tpu as pltpu
from jax.sharding import PartitionSpec as P

AXIAL_MACH = 0.4
STEP_SIZE = 0.3
MESH = pl.DeviceIdType.MESH


def build_table(index, weight):
    taps, width = index.shape
    normed = weight / jnp.sum(weight, axis=0, keepdims=True)
    source = lax.broadcasted_iota(jnp.int32, (width, width), 0)
    matrix = jnp.zeros((width, width), jnp.float32)
    for tap in range(taps):
        matrix += jnp.where(index[tap : tap + 1] == source, normed[tap : tap + 1], 0.0)
    high = matrix.astype(jnp.bfloat16)
    low = (matrix - high.astype(jnp.float32)).astype(jnp.bfloat16)
    top = jnp.concatenate([high, low], axis=1)
    bottom = jnp.concatenate([high, jnp.zeros_like(high)], axis=1)
    return jnp.concatenate([top, bottom], axis=0)


def interpolate(plane, table):
    width = plane.shape[1]
    high = plane.astype(jnp.bfloat16)
    low = (plane - high.astype(jnp.float32)).astype(jnp.bfloat16)
    both = jnp.dot(
        jnp.concatenate([high, low], axis=1), table, preferred_element_type=jnp.float32
    )
    return both[:, :width] + both[:, width:]


def kernel(
    n_circ, n_rad, odd, gap,
    state_hbm, eddy_hbm, offset_hbm, index_hbm, weight_hbm, out_ref,
    state_ref, eddy_ref, offset_ref, index_ref, weight_ref,
    field, slopes, total, table, plane_out, rad_bulk_out, rad_bulk_in, rad_front_out, rad_front_in,
    circ_out, circ_in,
    load_sem, plane_send, plane_recv, rad_send, rad_recv, circ_send, circ_recv, plane_in,
):
    nvar, naxial, nradial, width = state_ref.shape
    sections = offset_ref.shape[0]
    rows = nvar * nradial
    inner = naxial - 1
    circ, rad, ax = lax.axis_index("circ"), lax.axis_index("rad"), lax.axis_index("ax")
    far = 1 - ax
    circ_up, circ_down = lax.rem(circ + 1, n_circ), lax.rem(circ + n_circ - 1, n_circ)
    has_low, has_high = rad > 0, rad < n_rad - 1

    barrier = pltpu.get_barrier_semaphore()

    def greet(device):
        pl.semaphore_signal(barrier, inc=1, device_id=device, device_id_type=MESH)

    for apart in range(n_circ):
        greet((lax.rem(circ + apart, n_circ), rad, far))
    greet((circ_up, rad, ax))
    greet((circ_down, rad, ax))

    @pl.when(has_low)
    def _():
        greet((circ, rad - 1, ax))

    @pl.when(has_high)
    def _():
        greet((circ, rad + 1, ax))

    loads = [
        pltpu.make_async_copy(source, target, load_sem.at[i])
        for i, (source, target) in enumerate(
            (
                (state_hbm, state_ref),
                (eddy_hbm, eddy_ref),
                (offset_hbm, offset_ref),
                (index_hbm.at[ax], index_ref),
                (weight_hbm.at[ax], weight_ref),
            )
        )
    ]
    for load in loads:
        load.start()

    for side, missing in ((0, jnp.logical_not(has_low)), (1, jnp.logical_not(has_high))):

        @pl.when(missing)
        def _():
            for s in range(sections):
                rad_bulk_in[s, side] = jnp.zeros((inner * nvar, width), jnp.float32)
                rad_front_in[s, side] = jnp.zeros((nvar, width), jnp.float32)

    def axial(j):
        return jnp.where(ax == 0, j, naxial - 1 - j)

    def place(j):
        return pl.ds(j * rows, rows)

    def plane_at(s, j):
        return field[s, place(j), :].reshape(nvar, nradial, width)

    for load in loads:
        load.wait()
    for j in range(naxial):
        field[0, place(j), :] = state_ref[:, axial(j)].reshape(rows, width)
    plane_out[0] = field[0, place(inner), :]

    def lowest(s):
        if gap == 1:
            return 0
        parity = 0
        for section_id in odd:
            parity = jnp.where(s == section_id, 1, parity)
        return lax.rem(circ + parity, gap)

    def plane_copy(s, turn):
        slot = jnp.where(circ < n_circ // 2, n_circ // gap - 1 - turn, turn)
        return pltpu.make_async_remote_copy(
            src_ref=plane_out.at[s], dst_ref=plane_in.at[s, circ // gap],
            send_sem=plane_send.at[s, turn], recv_sem=plane_recv.at[s, circ // gap],
            device_id=(lowest(s) + gap * slot, rad, far), device_id_type=MESH,
        )

    def plane_arrival(s, slot):
        return pltpu.make_async_remote_copy(
            src_ref=plane_out.at[s], dst_ref=plane_in.at[s, slot],
            send_sem=plane_send.at[s, 0], recv_sem=plane_recv.at[s, slot],
            device_id=(lowest(s) + gap * slot, rad, far), device_id_type=MESH,
        )

    def circ_copy(s, part, side):
        return pltpu.make_async_remote_copy(
            src_ref=circ_out.at[s, part, side], dst_ref=circ_in.at[s, part, side],
            send_sem=circ_send.at[s, part, side], recv_sem=circ_recv.at[s, part, side],
            device_id=(circ_up if side == 0 else circ_down, rad, ax), device_id_type=MESH,
        )

    rad_outs, rad_ins = (rad_bulk_out, rad_front_out), (rad_bulk_in, rad_front_in)

    def rad_copy(s, part, side):
        return pltpu.make_async_remote_copy(
            src_ref=rad_outs[part].at[s, side], dst_ref=rad_ins[part].at[s, side],
            send_sem=rad_send.at[s, part, side], recv_sem=rad_recv.at[s, part, side],
            device_id=(circ, rad + 1 if side == 0 else rad - 1, ax), device_id_type=MESH,
        )

    sends_rad = (has_high, has_low)
    gets_rad = (has_low, has_high)
    spans = ((0, inner), (inner, naxial))

    def send_halos(s, part):
        first, stop = spans[part]
        tiles = (stop - first) * nvar
        cells = field[s, first * rows : stop * rows, :].reshape(tiles, nradial, width)
        lane_of = lax.broadcasted_iota(jnp.int32, cells.shape, 2)
        tile_of = lax.broadcasted_iota(jnp.int32, cells.shape, 0)
        for side, edge in ((0, width - 1), (1, 0)):
            column = jnp.broadcast_to(cells[:, :, edge : edge + 1], cells.shape)
            circ_out[s, part, side] = jnp.sum(jnp.where(lane_of == tile_of, column, 0.0), axis=0)
            circ_copy(s, part, side).start()
        for side, edge in ((0, nradial - 1), (1, 0)):
            start = first * rows + edge
            rad_outs[part][s, side] = field[s, pl.ds(start, tiles, stride=nradial), :]

            @pl.when(sends_rad[side])
            def _():
                rad_copy(s, part, side).start()

    def await_halos(s, part):
        for side in range(2):
            circ_copy(s, part, side).wait_recv()

            @pl.when(gets_rad[side])
            def _():
                rad_copy(s, part, side).wait_recv()

    lane = lax.broadcasted_iota(jnp.int32, (nvar, nradial, width), 2)
    sub = lax.broadcasted_iota(jnp.int32, (nvar, nradial, width), 1)
    zero = jnp.zeros((nvar, nradial, width), jnp.float32)
    swirl = jnp.where(ax == 1, -0.3, 0.2).astype(jnp.float32)
    toward = jnp.where(ax == 1, -0.5, 0.5).astype(jnp.float32)

    at_low, at_high = lane[0] == 0, lane[0] == width - 1
    at_under, at_over = sub[0] == 0, sub[0] == nradial - 1
    half = lambda where: jnp.where(where, 0.5, 0.0).astype(jnp.float32)
    half_low, half_high, half_under, half_over = map(half, (at_low, at_high, at_under, at_over))

    def inside(s, j):
        q = plane_at(s, j)
        before = plane_at(s, j - 1) if j > 0 else zero
        after = plane_at(s, j + 1) if j < inner else zero
        circ_low = jnp.where(lane == 0, 0.0, pltpu.roll(q, 1, 2))
        circ_high = jnp.where(lane == width - 1, 0.0, pltpu.roll(q, width - 1, 2))
        rad_low = jnp.where(sub == 0, 0.0, pltpu.roll(q, 1, 1))
        rad_high = jnp.where(sub == nradial - 1, 0.0, pltpu.roll(q, nradial - 1, 1))
        diff_circ = 0.5 * (circ_high - circ_low)
        diff_axial = toward * (after - before)
        laplace = (circ_high + circ_low) + (rad_high + rad_low) + (after + before) - 6.0 * q
        slope = eddy_ref[axial(j)][None] * laplace - (swirl * diff_circ + AXIAL_MACH * diff_axial)
        diverge = diff_circ[1] + 0.5 * (rad_high[2] - rad_low[2]) + diff_axial[3]
        push = 0.5 * (rad_high[4] - rad_low[4])
        return slope - jnp.stack([diverge, diff_circ[4], push, diff_axial[4], diverge])

    def from_halos(s, j, part, edges):
        first = (j - spans[part][0]) * nvar
        eddy = eddy_ref[axial(j)]
        by_low = jnp.where(at_low, eddy + 0.5 * swirl, 0.0)
        by_high = jnp.where(at_high, eddy - 0.5 * swirl, 0.0)
        by_under = jnp.where(at_under, eddy, 0.0)
        by_over = jnp.where(at_over, eddy, 0.0)

        def column(side, v):
            t = first + v
            return jnp.broadcast_to(edges[side][:, t : t + 1], (nradial, width))

        def row(side, v):
            picked = rad_ins[part][s, side, first + v : first + v + 1, :]
            return jnp.broadcast_to(picked, (nradial, width))

        low, high = ([column(side, v) for v in range(nvar)] for side in range(2))
        under, over = ([row(side, v) for v in range(nvar)] for side in range(2))
        added = [
            (by_low * low[v] + by_high * high[v]) + (by_under * under[v] + by_over * over[v])
            for v in range(nvar)
        ]
        spread = (half_low * low[1] - half_high * high[1]) + (
            half_under * under[2] - half_over * over[2]
        )
        added[0] += spread
        added[1] += half_low * low[4] - half_high * high[4]
        added[2] += half_under * under[4] - half_over * over[4]
        added[4] += spread
        return jnp.stack(added)

    def advance(s, j, slope):
        blend = jnp.where((s == 0) | (s == sections - 1), 1.0, 2.0).astype(jnp.float32)
        reach = jnp.where(s < sections - 2, 0.5 * STEP_SIZE, STEP_SIZE).astype(jnp.float32)
        total[j] += blend * slope
        ahead = (plane_at(0, j) + reach * slope).reshape(rows, width)
        field[s + 1, place(j), :] = ahead
        if j == inner:
            plane_out[s + 1] = ahead

    def send_planes(s):
        for turn in range(n_circ // gap):
            plane_copy(s, turn).start()

    arrivals = n_circ + 2 + jnp.where(has_low, 1, 0) + jnp.where(has_high, 1, 0)
    pl.semaphore_wait(barrier, arrivals)
    send_planes(0)
    send_halos(0, 1)
    send_halos(0, 0)

    def section(s, carry):
        table[s] = build_table(index_ref[s], weight_ref[s])
        for j in range(naxial):
            slopes[j] = inside(s, j)
        await_halos(s, 0)
        edges = [circ_in[s, 0, side] for side in range(2)]
        for j in range(inner):
            advance(s, j, slopes[j] + from_halos(s, j, 0, edges))

        @pl.when(s < sections - 1)
        def _():
            send_halos(s + 1, 0)

        await_halos(s, 1)
        edges = [circ_in[s, 1, side] for side in range(2)]
        slope = slopes[inner] + from_halos(s, inner, 1, edges)
        for slot in range(n_circ // gap):
            plane_arrival(s, slot).wait_recv()
        shift = jnp.where(ax == 1, offset_ref[s], n_circ - offset_ref[s])
        facing = lax.rem(circ + shift, n_circ) // gap
        faced = plane_in[s, 0]
        for slot in range(1, n_circ // gap):
            faced = jnp.where(facing == slot, plane_in[s, slot], faced)
        ghost = interpolate(faced, table[s]).reshape(nvar, nradial, width)
        slant = toward * ghost
        none = jnp.zeros_like(slant[0])
        slope = slope + eddy_ref[axial(inner)][None] * ghost - AXIAL_MACH * slant
        slope = slope - jnp.stack([slant[3], none, none, slant[4], slant[3]])
        advance(s, inner, slope)

        @pl.when(s < sections - 1)
        def _():
            send_planes(s + 1)
            send_halos(s + 1, 1)

        return carry

    total[...] = jnp.zeros_like(total)
    lax.fori_loop(0, sections, section, 0)

    for j in range(naxial):
        out_ref[:, axial(j)] = plane_at(0, j) + (STEP_SIZE / 6.0) * total[j]

    def finish(s, carry):
        for turn in range(n_circ // gap):
            plane_copy(s, turn).wait_send()
        for part in range(2):
            for side in range(2):
                circ_copy(s, part, side).wait_send()

                @pl.when(sends_rad[side])
                def _():
                    rad_copy(s, part, side).wait_send()

        return carry

    lax.fori_loop(0, sections, finish, 0)


def solution(mesh):
    n_circ, n_rad = mesh.shape["circ"], mesh.shape["rad"]

    def variant(odd, gap, label, state, eddy, offsets, stencil_index, stencil_weight):
        nvar, naxial, nradial, width = state.shape
        sections = offsets.shape[0]
        taps = stencil_index.shape[3]
        rows, inner = nvar * nradial, naxial - 1
        whole = pl.BlockSpec(memory_space=pltpu.HBM)
        buffer = lambda *shape: pltpu.VMEM(shape, jnp.float32)
        copies = lambda *shape: pltpu.SemaphoreType.DMA(shape)
        return pl.pallas_call(
            functools.partial(kernel, n_circ, n_rad, odd, gap),
            out_shape=pltpu.VMEM(state.shape, jnp.float32),
            in_specs=[whole] * 5,
            out_specs=pl.BlockSpec(memory_space=pltpu.VMEM),
            scratch_shapes=[
                buffer(*state.shape),
                buffer(*eddy.shape),
                pltpu.SMEM((sections,), jnp.int32),
                pltpu.VMEM((sections, taps, width), jnp.int32),
                buffer(sections, taps, width),
                buffer(sections + 1, rows * naxial, width),
                buffer(naxial, nvar, nradial, width),
                buffer(naxial, nvar, nradial, width),
                pltpu.VMEM((sections, 2 * width, 2 * width), jnp.bfloat16),
                buffer(sections + 1, rows, width),
                buffer(sections, 2, inner * nvar, width),
                buffer(sections, 2, inner * nvar, width),
                buffer(sections, 2, nvar, width),
                buffer(sections, 2, nvar, width),
                buffer(sections, 2, 2, nradial, width),
                buffer(sections, 2, 2, nradial, width),
                copies(5),
                copies(sections, n_circ // gap),
                copies(sections, n_circ // gap),
                copies(sections, 2, 2),
                copies(sections, 2, 2),
                copies(sections, 2, 2),
                copies(sections, 2, 2),
                buffer(sections, n_circ // gap, rows, width),
            ],
            compiler_params=pltpu.CompilerParams(
                collective_id=label, has_side_effects=True, vmem_limit_bytes=60 * 1024 * 1024
            ),
        )(state, eddy, offsets, jnp.swapaxes(stencil_index, 2, 3), jnp.swapaxes(stencil_weight, 2, 3))

    def local(state, eddy, offsets, stencil_index, stencil_weight):
        operands = (state, eddy, offsets, stencil_index, stencil_weight)
        sections = offsets.shape[0]
        if n_circ % 4:
            return variant((), 1, 0, *operands)
        patterns = [
            odd
            for count in range(1, sections - 1)
            for odd in itertools.combinations(range(sections), count)
        ]
        codes = [sum(1 << s for s in odd) for odd in patterns]
        code = sum((offsets[s] % 2) * (1 << s) for s in range(sections))
        chosen = sum(jnp.where(code == each, i, 0) for i, each in enumerate(codes))
        branches = [functools.partial(variant, odd, 2, i) for i, odd in enumerate(patterns)]
        return lax.switch(chosen, branches, *operands)

    return jax.shard_map(
        local,
        mesh=mesh,
        in_specs=(P(None, "ax", "rad", "circ"), P("ax", "rad", "circ"), P(), P(), P()),
        out_specs=P(None, "ax", "rad", "circ"),
        check_vma=False,
    )
```

```python
import functools

import jax
import jax.numpy as jnp
from jax import lax
from jax.experimental import pallas as pl
from jax.experimental.pallas import tpu as pltpu
from jax.sharding import PartitionSpec as P

AXIAL_MACH = 0.4
STEP_SIZE = 0.3
MESH = pl.DeviceIdType.MESH


def build_table(index, weight):
    taps, width = index.shape
    normed = weight / jnp.sum(weight, axis=0, keepdims=True)
    source = lax.broadcasted_iota(jnp.int32, (width, width), 0)
    matrix = jnp.zeros((width, width), jnp.float32)
    for tap in range(taps):
        matrix += jnp.where(index[tap : tap + 1] == source, normed[tap : tap + 1], 0.0)
    high = matrix.astype(jnp.bfloat16)
    low = (matrix - high.astype(jnp.float32)).astype(jnp.bfloat16)
    top = jnp.concatenate([high, low], axis=1)
    bottom = jnp.concatenate([high, jnp.zeros_like(high)], axis=1)
    return jnp.concatenate([top, bottom], axis=0)


def interpolate(plane, table):
    width = plane.shape[1]
    high = plane.astype(jnp.bfloat16)
    low = (plane - high.astype(jnp.float32)).astype(jnp.bfloat16)
    both = jnp.dot(
        jnp.concatenate([high, low], axis=1), table, preferred_element_type=jnp.float32
    )
    return both[:, :width] + both[:, width:]


def kernel(
    n_circ, n_rad,
    state_hbm, eddy_hbm, offset_hbm, index_hbm, weight_hbm, out_ref,
    state_ref, eddy_ref, offset_ref, index_ref, weight_ref,
    field, slopes, total, table, plane_out, rad_bulk_out, rad_bulk_in, rad_front_out, rad_front_in,
    circ_out, circ_in,
    load_sem, plane_send, plane_recv, rad_send, rad_recv, circ_send, circ_recv, plane_in,
):
    nvar, naxial, nradial, width = state_ref.shape
    sections = offset_ref.shape[0]
    rows = nvar * nradial
    inner = naxial - 1
    circ, rad, ax = lax.axis_index("circ"), lax.axis_index("rad"), lax.axis_index("ax")
    far = 1 - ax
    circ_up, circ_down = lax.rem(circ + 1, n_circ), lax.rem(circ + n_circ - 1, n_circ)
    has_low, has_high = rad > 0, rad < n_rad - 1

    barrier = pltpu.get_barrier_semaphore()

    def greet(device):
        pl.semaphore_signal(barrier, inc=1, device_id=device, device_id_type=MESH)

    for apart in range(n_circ):
        greet((lax.rem(circ + apart, n_circ), rad, far))
    greet((circ_up, rad, ax))
    greet((circ_down, rad, ax))

    @pl.when(has_low)
    def _():
        greet((circ, rad - 1, ax))

    @pl.when(has_high)
    def _():
        greet((circ, rad + 1, ax))

    loads = [
        pltpu.make_async_copy(source, target, load_sem.at[i])
        for i, (source, target) in enumerate(
            (
                (state_hbm, state_ref),
                (eddy_hbm, eddy_ref),
                (offset_hbm, offset_ref),
                (index_hbm.at[ax], index_ref),
                (weight_hbm.at[ax], weight_ref),
            )
        )
    ]
    for load in loads:
        load.start()

    for side, missing in ((0, jnp.logical_not(has_low)), (1, jnp.logical_not(has_high))):

        @pl.when(missing)
        def _():
            for s in range(sections):
                rad_bulk_in[s, side] = jnp.zeros((inner * nvar, width), jnp.float32)
                rad_front_in[s, side] = jnp.zeros((nvar, width), jnp.float32)

    def axial(j):
        return jnp.where(ax == 0, j, naxial - 1 - j)

    def place(j):
        return pl.ds(j * rows, rows)

    def plane_at(s, j):
        return field[s, place(j), :].reshape(nvar, nradial, width)

    for load in loads:
        load.wait()
    for j in range(naxial):
        field[0, place(j), :] = state_ref[:, axial(j)].reshape(rows, width)
    plane_out[0] = field[0, place(inner), :]

    def plane_copy(s, turn):
        target = jnp.where(circ < n_circ // 2, n_circ - 1 - turn, turn)
        return pltpu.make_async_remote_copy(
            src_ref=plane_out.at[s], dst_ref=plane_in.at[s, circ],
            send_sem=plane_send.at[s, turn], recv_sem=plane_recv.at[s, circ],
            device_id=(target, rad, far), device_id_type=MESH,
        )

    def plane_arrival(s, source):
        return pltpu.make_async_remote_copy(
            src_ref=plane_out.at[s], dst_ref=plane_in.at[s, source],
            send_sem=plane_send.at[s, 0], recv_sem=plane_recv.at[s, source],
            device_id=(source, rad, far), device_id_type=MESH,
        )

    def circ_copy(s, part, side):
        return pltpu.make_async_remote_copy(
            src_ref=circ_out.at[s, part, side], dst_ref=circ_in.at[s, part, side],
            send_sem=circ_send.at[s, part, side], recv_sem=circ_recv.at[s, part, side],
            device_id=(circ_up if side == 0 else circ_down, rad, ax), device_id_type=MESH,
        )

    rad_outs, rad_ins = (rad_bulk_out, rad_front_out), (rad_bulk_in, rad_front_in)

    def rad_copy(s, part, side):
        return pltpu.make_async_remote_copy(
            src_ref=rad_outs[part].at[s, side], dst_ref=rad_ins[part].at[s, side],
            send_sem=rad_send.at[s, part, side], recv_sem=rad_recv.at[s, part, side],
            device_id=(circ, rad + 1 if side == 0 else rad - 1, ax), device_id_type=MESH,
        )

    sends_rad = (has_high, has_low)
    gets_rad = (has_low, has_high)
    spans = ((0, inner), (inner, naxial))

    def send_halos(s, part):
        first, stop = spans[part]
        tiles = (stop - first) * nvar
        cells = field[s, first * rows : stop * rows, :].reshape(tiles, nradial, width)
        lane_of = lax.broadcasted_iota(jnp.int32, cells.shape, 2)
        tile_of = lax.broadcasted_iota(jnp.int32, cells.shape, 0)
        for side, edge in ((0, width - 1), (1, 0)):
            column = jnp.broadcast_to(cells[:, :, edge : edge + 1], cells.shape)
            circ_out[s, part, side] = jnp.sum(jnp.where(lane_of == tile_of, column, 0.0), axis=0)
            circ_copy(s, part, side).start()
        for side, edge in ((0, nradial - 1), (1, 0)):
            start = first * rows + edge
            rad_outs[part][s, side] = field[s, pl.ds(start, tiles, stride=nradial), :]

            @pl.when(sends_rad[side])
            def _():
                rad_copy(s, part, side).start()

    def await_halos(s, part):
        for side in range(2):
            circ_copy(s, part, side).wait_recv()

            @pl.when(gets_rad[side])
            def _():
                rad_copy(s, part, side).wait_recv()

    lane = lax.broadcasted_iota(jnp.int32, (nvar, nradial, width), 2)
    sub = lax.broadcasted_iota(jnp.int32, (nvar, nradial, width), 1)
    zero = jnp.zeros((nvar, nradial, width), jnp.float32)
    swirl = jnp.where(ax == 1, -0.3, 0.2).astype(jnp.float32)
    toward = jnp.where(ax == 1, -0.5, 0.5).astype(jnp.float32)

    at_low, at_high = lane[0] == 0, lane[0] == width - 1
    at_under, at_over = sub[0] == 0, sub[0] == nradial - 1
    half = lambda where: jnp.where(where, 0.5, 0.0).astype(jnp.float32)
    half_low, half_high, half_under, half_over = map(half, (at_low, at_high, at_under, at_over))

    def inside(s, j):
        q = plane_at(s, j)
        before = plane_at(s, j - 1) if j > 0 else zero
        after = plane_at(s, j + 1) if j < inner else zero
        circ_low = jnp.where(lane == 0, 0.0, pltpu.roll(q, 1, 2))
        circ_high = jnp.where(lane == width - 1, 0.0, pltpu.roll(q, width - 1, 2))
        rad_low = jnp.where(sub == 0, 0.0, pltpu.roll(q, 1, 1))
        rad_high = jnp.where(sub == nradial - 1, 0.0, pltpu.roll(q, nradial - 1, 1))
        diff_circ = 0.5 * (circ_high - circ_low)
        diff_axial = toward * (after - before)
        laplace = (circ_high + circ_low) + (rad_high + rad_low) + (after + before) - 6.0 * q
        slope = eddy_ref[axial(j)][None] * laplace - (swirl * diff_circ + AXIAL_MACH * diff_axial)
        diverge = diff_circ[1] + 0.5 * (rad_high[2] - rad_low[2]) + diff_axial[3]
        push = 0.5 * (rad_high[4] - rad_low[4])
        return slope - jnp.stack([diverge, diff_circ[4], push, diff_axial[4], diverge])

    def from_halos(s, j, part, edges):
        first = (j - spans[part][0]) * nvar
        eddy = eddy_ref[axial(j)]
        by_low = jnp.where(at_low, eddy + 0.5 * swirl, 0.0)
        by_high = jnp.where(at_high, eddy - 0.5 * swirl, 0.0)
        by_under = jnp.where(at_under, eddy, 0.0)
        by_over = jnp.where(at_over, eddy, 0.0)

        def column(side, v):
            t = first + v
            return jnp.broadcast_to(edges[side][:, t : t + 1], (nradial, width))

        def row(side, v):
            picked = rad_ins[part][s, side, first + v : first + v + 1, :]
            return jnp.broadcast_to(picked, (nradial, width))

        low, high = ([column(side, v) for v in range(nvar)] for side in range(2))
        under, over = ([row(side, v) for v in range(nvar)] for side in range(2))
        added = [
            (by_low * low[v] + by_high * high[v]) + (by_under * under[v] + by_over * over[v])
            for v in range(nvar)
        ]
        spread = (half_low * low[1] - half_high * high[1]) + (
            half_under * under[2] - half_over * over[2]
        )
        added[0] += spread
        added[1] += half_low * low[4] - half_high * high[4]
        added[2] += half_under * under[4] - half_over * over[4]
        added[4] += spread
        return jnp.stack(added)

    def advance(s, j, slope):
        blend = jnp.where((s == 0) | (s == sections - 1), 1.0, 2.0).astype(jnp.float32)
        reach = jnp.where(s < sections - 2, 0.5 * STEP_SIZE, STEP_SIZE).astype(jnp.float32)
        total[j] += blend * slope
        ahead = (plane_at(0, j) + reach * slope).reshape(rows, width)
        field[s + 1, place(j), :] = ahead
        if j == inner:
            plane_out[s + 1] = ahead

    def send_planes(s):
        for turn in range(n_circ):
            plane_copy(s, turn).start()

    arrivals = n_circ + 2 + jnp.where(has_low, 1, 0) + jnp.where(has_high, 1, 0)
    pl.semaphore_wait(barrier, arrivals)
    send_planes(0)
    send_halos(0, 1)
    send_halos(0, 0)

    def section(s, carry):
        table[s] = build_table(index_ref[s], weight_ref[s])
        for j in range(naxial):
            slopes[j] = inside(s, j)
        await_halos(s, 0)
        edges = [circ_in[s, 0, side] for side in range(2)]
        for j in range(inner):
            advance(s, j, slopes[j] + from_halos(s, j, 0, edges))

        await_halos(s, 1)
        edges = [circ_in[s, 1, side] for side in range(2)]
        slope = slopes[inner] + from_halos(s, inner, 1, edges)
        for source in range(n_circ):
            plane_arrival(s, source).wait_recv()
        shift = jnp.where(ax == 1, offset_ref[s], n_circ - offset_ref[s])
        facing = lax.rem(circ + shift, n_circ)
        faced = plane_in[s, 0]
        for source in range(1, n_circ):
            faced = jnp.where(facing == source, plane_in[s, source], faced)
        ghost = interpolate(faced, table[s]).reshape(nvar, nradial, width)
        slant = toward * ghost
        none = jnp.zeros_like(slant[0])
        slope = slope + eddy_ref[axial(inner)][None] * ghost - AXIAL_MACH * slant
        slope = slope - jnp.stack([slant[3], none, none, slant[4], slant[3]])
        advance(s, inner, slope)

        @pl.when(s < sections - 1)
        def _():
            send_planes(s + 1)
            send_halos(s + 1, 1)
            send_halos(s + 1, 0)

        return carry

    total[...] = jnp.zeros_like(total)
    lax.fori_loop(0, sections, section, 0)

    for j in range(naxial):
        out_ref[:, axial(j)] = plane_at(0, j) + (STEP_SIZE / 6.0) * total[j]

    def finish(s, carry):
        for turn in range(n_circ):
            plane_copy(s, turn).wait_send()
        for part in range(2):
            for side in range(2):
                circ_copy(s, part, side).wait_send()

                @pl.when(sends_rad[side])
                def _():
                    rad_copy(s, part, side).wait_send()

        return carry

    lax.fori_loop(0, sections, finish, 0)


def solution(mesh):
    n_circ, n_rad = mesh.shape["circ"], mesh.shape["rad"]

    def local(state, eddy, offsets, stencil_index, stencil_weight):
        nvar, naxial, nradial, width = state.shape
        sections = offsets.shape[0]
        taps = stencil_index.shape[3]
        rows, inner = nvar * nradial, naxial - 1
        whole = pl.BlockSpec(memory_space=pltpu.HBM)
        buffer = lambda *shape: pltpu.VMEM(shape, jnp.float32)
        copies = lambda *shape: pltpu.SemaphoreType.DMA(shape)
        step = pl.pallas_call(
            functools.partial(kernel, n_circ, n_rad),
            out_shape=pltpu.VMEM(state.shape, jnp.float32),
            in_specs=[whole] * 5,
            out_specs=pl.BlockSpec(memory_space=pltpu.VMEM),
            scratch_shapes=[
                buffer(*state.shape),
                buffer(*eddy.shape),
                pltpu.SMEM((sections,), jnp.int32),
                pltpu.VMEM((sections, taps, width), jnp.int32),
                buffer(sections, taps, width),
                buffer(sections + 1, rows * naxial, width),
                buffer(naxial, nvar, nradial, width),
                buffer(naxial, nvar, nradial, width),
                pltpu.VMEM((sections, 2 * width, 2 * width), jnp.bfloat16),
                buffer(sections + 1, rows, width),
                buffer(sections, 2, inner * nvar, width),
                buffer(sections, 2, inner * nvar, width),
                buffer(sections, 2, nvar, width),
                buffer(sections, 2, nvar, width),
                buffer(sections, 2, 2, nradial, width),
                buffer(sections, 2, 2, nradial, width),
                copies(5),
                copies(sections, n_circ),
                copies(sections, n_circ),
                copies(sections, 2, 2),
                copies(sections, 2, 2),
                copies(sections, 2, 2),
                copies(sections, 2, 2),
                buffer(sections, n_circ, rows, width),
            ],
            compiler_params=pltpu.CompilerParams(
                collective_id=0, has_side_effects=True, vmem_limit_bytes=60 * 1024 * 1024
            ),
        )(state, eddy, offsets, jnp.swapaxes(stencil_index, 2, 3), jnp.swapaxes(stencil_weight, 2, 3))
        return step

    return jax.shard_map(
        local,
        mesh=mesh,
        in_specs=(P(None, "ax", "rad", "circ"), P("ax", "rad", "circ"), P(), P(), P()),
        out_specs=P(None, "ax", "rad", "circ"),
        check_vma=False,
    )
```
